128 devices in a mesh: gx: 16 (over y, z), gy: 8 (over x, core).
Axes of the slice: x: 4, y: 4, z: 4, core: 2. Of those that a mesh axis runs over, the one named last changes fastest.
Arguments:
- next_adjoint: float32 [4, 256, 128, 1024], P(None, 'gx', 'gy'), may hold values from -6 to 6
- accumulation: float32 [256, 128, 1024], P('gx', 'gy'), may hold values from 0.5 to 5
- trans_x: float32 [256, 128, 1024], P('gx', 'gy'), may hold values from 0.1 to 2
- trans_y: float32 [256, 128, 1024], P('gx', 'gy'), may hold values from 0.1 to 2
- trans_z: float32 [256, 128, 1024], P('gx', 'gy'), may hold values from 0.1 to 2
- well_owner: int32 [8192, 1], P(('gx', 'gy')), may hold values from 0 to 127; in each aligned block of 64 rows (0 to 63, 64 to 127, ...) no two rows name the same one
- well_site: int32 [8192], P(('gx', 'gy')), may hold values from 0 to 255
- perf_layers: int32 [8192, 16], P(('gx', 'gy')), may hold values from 0 to 1023
- perf_count: int32 [8192], P(('gx', 'gy')), may hold values from 1 to 16
- well_index: float32 [8192, 16], P(('gx', 'gy')), may hold values from 0.5 to 5
- misfit: float32 [8192, 4], P(('gx', 'gy')), may hold values from -6 to 6
Outputs:
- adjoint_field: float32 [4, 256, 128, 1024], P(None, 'gx', 'gy')
- residual: float32 [4, 256, 128, 1024], P(None, 'gx', 'gy')
The draws below stay inside these ranges and needn't reach their ends.
Inputs may be any that keep to these rules, and one draw needn't show every extreme that they name: `well_owner`: device number d stands at gx index d // (devices along gy) and gy index d % (devices along gy). In each aligned block of 64 rows (the wells of one device) at most 1 row name the same device. The column's offsets in the owner's block are well_site // 16 along the first dimension and well_site % 16 along the second. The first perf_count[w] entries of row w of perf_layers and well_index are the well's perforations; the rest are unused.
All inputs are finite; a program needn't handle non-finite values.
Results may differ from the reference program's by a relative error of at most 0.038.
Values sent between devices are 32-bit elements; how exact they have to be, the bound alone decides.
A program may use at most 320 MiB of HBM per device.

```python
import math
import jax
import jax.numpy as jnp
import numpy as np
from jax import lax

K = 4
CX = 16
CY = 16
NZ = 1024
W_DEV = 64
CAP = 1
PERF = 16
ITERS = 2
NX = 256
NY = 128
WELLS = 8192
N_GX = 16
N_GY = 8


def plant(values, rng, smallest, largest):
    dims = values.shape
    index_at = [jax.random.randint(jax.random.fold_in(rng, axis), (), 0, dims[axis]) for axis in range(len(dims))]
    values = values.at[tuple(index_at)].set(smallest)
    longest = dims.index(max(dims))
    index_at[longest] = (index_at[longest] + 1) % dims[longest]
    return values.at[tuple(index_at)].set(largest)


def block_levels(rng, extent, split, smallest, top_value):
    factor_of, own = 1.0, jax.random.fold_in(rng, 6)
    for position, parts in split:
        steps = jnp.exp(jax.random.uniform(jax.random.fold_in(own, position), (parts,), jnp.float32, smallest / len(split), top_value / len(split)))
        factor_of = factor_of * jnp.repeat(steps, extent[position] // parts).reshape([-1 if axis == position else 1 for axis in range(len(extent))])
    return factor_of


def deal_out(key, own, number, rows, count, top, most, skew):
    order = jax.random.permutation(key, count)
    packed, ordinary = load_shares(count, rows * top, most, skew, True), load_shares(count, rows * top, most, skew, False)
    places = jnp.arange(count)

    def named(tallies, turn):
        used = int((tallies > 0).sum())
        fixed = max(1, used // 4)
        moved = fixed + (places - fixed + turn * (used - fixed)) % max(1, count - fixed)
        return jnp.zeros((count,), jnp.int32).at[order[jnp.where(places < fixed, places, moved)]].set(jnp.asarray(tallies, jnp.int32))

    tallies = jnp.where(number % 4 == 0, named(packed, number // 4), named(ordinary, number - number // 4 - 1))
    mixed = jax.random.permutation(jax.random.fold_in(own, 3), count)
    giver, receiver = mixed[0:count // 2 * 2:2], mixed[1:count // 2 * 2:2]
    margin = jnp.minimum(tallies[giver] - 1, most - tallies[receiver]) // 2
    margin = jnp.where((giver == order[0]) | (receiver == order[0]) | (tallies[receiver] == 0), 0, jnp.maximum(margin, 0))
    moved = jax.random.randint(jax.random.fold_in(own, 4), (count // 2,), 0, 1 << 20) % (margin + 1)
    tallies = tallies.at[giver].add(-moved).at[receiver].add(moved)
    items = jnp.searchsorted(jnp.cumsum(tallies), jnp.arange(rows * top), side="right").astype(jnp.int32)
    listing = items.reshape(top, rows).T
    listing = listing[jax.random.permutation(jax.random.fold_in(own, 1), rows)]
    turn = jax.random.randint(jax.random.fold_in(own, 2), (rows, 1), 0, top)
    return jnp.take_along_axis(listing, (jnp.arange(top)[None, :] + turn) % top, axis=1)


def load_shares(count, total, bound, skew, full):
    weights = [(1 << 20) // math.isqrt(standing ** skew) + 1 for standing in range(1, count + 1)]
    largest = bound if full else min(bound, max(-(-total // count), total * weights[0] // sum(weights)))
    least = 1 if total - largest >= count - 1 else 0
    given, surplus = [largest] + [least] * (count - 1), total - largest - least * (count - 1)
    while surplus > 0:
        candidates = [i for i in range(1, count) if given[i] < largest] or [i for i in range(1, count) if given[i] < bound]
        whole, left = sum([weights[i] for i in candidates]), surplus
        for i in candidates:
            more = min(bound - given[i], max(1, left * weights[i] // whole), surplus)
            given[i] = given[i] + more
            surplus = surplus - more
    return np.array(given)


def normal_values(stream_key, shape, deviation, bound, pieces=(), dtype=jnp.bfloat16):
    values = deviation * jax.random.normal(stream_key, shape, jnp.float32)
    if pieces:
        values = values * block_levels(stream_key, shape, pieces, -0.22, 0.18)
    return jnp.clip(values, -bound, bound).astype(dtype)


def setup_inputs(seed: int = 0) -> dict:
    streams_of = jax.random.split(jax.random.key(seed), 12)
    next_adjoint = normal_values(streams_of[0], (K, NX, NY, NZ), 1.0, 6.0, ((1, 16), (2, 8)), jnp.float32)
    accumulation = jnp.clip(jnp.exp(math.log(5.0) - 2.3025851 * jax.random.uniform(streams_of[1], (NX, NY, NZ), jnp.float32) ** block_levels(streams_of[1], (NX, NY, NZ), ((0, 16), (1, 8)), -0.2, 0.2)), 0.5, 5.0)
    trans_x = jnp.clip(jnp.exp(math.log(2.0) - 2.9957323 * jax.random.uniform(streams_of[2], (NX, NY, NZ), jnp.float32) ** block_levels(streams_of[2], (NX, NY, NZ), ((0, 16), (1, 8)), -0.2, 0.2)), 0.1, 2.0)
    trans_y = jnp.clip(jnp.exp(math.log(2.0) - 2.9957323 * jax.random.uniform(streams_of[3], (NX, NY, NZ), jnp.float32) ** block_levels(streams_of[3], (NX, NY, NZ), ((0, 16), (1, 8)), -0.2, 0.2)), 0.1, 2.0)
    trans_z = jnp.clip(jnp.exp(math.log(2.0) - 2.9957323 * jax.random.uniform(streams_of[4], (NX, NY, NZ), jnp.float32) ** block_levels(streams_of[4], (NX, NY, NZ), ((0, 16), (1, 8)), -0.2, 0.2)), 0.1, 2.0)
    well_owner_keys = jax.random.split(jax.random.fold_in(streams_of[5], 1), WELLS // W_DEV)
    well_owner_turns = jax.random.permutation(jax.random.fold_in(streams_of[5], 3), WELLS // W_DEV)
    well_owner = jax.vmap(lambda own, number: deal_out(jax.random.fold_in(streams_of[5], 2), own, number, W_DEV, N_GX * N_GY, 1, CAP, 2))(well_owner_keys, well_owner_turns).reshape((WELLS, 1))
    well_site = plant(jax.random.randint(streams_of[6], (WELLS,), 0, CX * CY), jax.random.fold_in(streams_of[6], 1), 0, (CX * CY) - 1).astype(jnp.int32)
    perf_layers = plant(jax.random.randint(streams_of[7], (WELLS, PERF), 0, NZ), jax.random.fold_in(streams_of[7], 1), 0, NZ - 1).astype(jnp.int32)
    perf_count = plant(jax.random.randint(streams_of[8], (WELLS,), 1, PERF + 1), jax.random.fold_in(streams_of[8], 1), 1, PERF).astype(jnp.int32)
    well_index = jnp.clip(jnp.exp(math.log(5.0) - 2.3025851 * jax.random.uniform(streams_of[9], (WELLS, PERF), jnp.float32) ** block_levels(streams_of[9], (WELLS, PERF), ((0, 128),), -0.2, 0.2)), 0.5, 5.0)
    misfit = normal_values(streams_of[10], (WELLS, K), 1.0, 6.0, ((0, 128),), jnp.float32)
    return {"next_adjoint": next_adjoint, "accumulation": accumulation, "trans_x": trans_x, "trans_y": trans_y, "trans_z": trans_z, "well_owner": well_owner, "well_site": well_site, "perf_layers": perf_layers, "perf_count": perf_count, "well_index": well_index, "misfit": misfit}


def well_terms(well_index, misfit, perf_count):
    active = (lax.broadcasted_iota(jnp.int32, well_index.shape, 1) < perf_count[:, None]).astype(jnp.float32)
    return misfit[:, :, None] * (well_index * active)[:, None, :]


def operate(field, accumulation, trans_x, trans_y, trans_z):
    up_x = jnp.concatenate([field[1:], jnp.zeros_like(field[:1])], axis=0)
    flux_x = trans_x * (up_x - field)
    lower_x = jnp.concatenate([jnp.zeros_like(flux_x[:1]), flux_x[:-1]], axis=0)
    up_y = jnp.concatenate([field[:, 1:], jnp.zeros_like(field[:, :1])], axis=1)
    flux_y = trans_y * (up_y - field)
    lower_y = jnp.concatenate([jnp.zeros_like(flux_y[:, :1]), flux_y[:, :-1]], axis=1)
    up_z = jnp.concatenate([field[..., 1:], jnp.zeros_like(field[..., :1])], axis=2)
    flux_z = trans_z * (up_z - field)
    lower_z = jnp.concatenate([jnp.zeros_like(flux_z[..., :1]), flux_z[..., :-1]], axis=2)
    return accumulation * field - flux_x + lower_x - flux_y + lower_y - flux_z + lower_z


def solve_one(right_side, accumulation, trans_x, trans_y, trans_z):
    solution = jnp.zeros_like(right_side)
    residual = right_side
    direction = right_side
    norm_now = jnp.sum(residual * residual)
    for turn_index in range(ITERS):
        image = operate(direction, accumulation, trans_x, trans_y, trans_z)
        step_len = norm_now / jnp.sum(direction * image)
        solution = solution + step_len * direction
        residual = residual - step_len * image
        norm_next = jnp.sum(residual * residual)
        direction = residual + (norm_next / norm_now) * direction
        norm_now = norm_next
    return solution, residual


def reference(next_adjoint, accumulation, trans_x, trans_y, trans_z, well_owner, well_site, perf_layers, perf_count, well_index, misfit):
    grid_shape = (NX, NY, NZ)
    plane_x = lax.broadcasted_iota(jnp.int32, grid_shape, 0)
    plane_y = lax.broadcasted_iota(jnp.int32, grid_shape, 1)
    plane_z = lax.broadcasted_iota(jnp.int32, grid_shape, 2)
    tx_eff = jnp.where(plane_x == NX - 1, jnp.float32(0.0), trans_x)
    ty_eff = jnp.where(plane_y == NY - 1, jnp.float32(0.0), trans_y)
    tz_eff = jnp.where(plane_z == NZ - 1, jnp.float32(0.0), trans_z)
    contrib = well_terms(well_index, misfit, perf_count)
    targets = well_owner[:, 0]
    cell_x = (targets // N_GY) * CX + well_site // CY
    cell_y = (targets % N_GY) * CY + well_site % CY
    cell_ids = ((cell_x * NY + cell_y) * NZ)[:, None] + perf_layers
    flat_vals = jnp.transpose(contrib, (1, 0, 2)).reshape(K, -1)
    sources = jnp.zeros((K, NX * NY * NZ), jnp.float32).at[:, cell_ids.reshape(-1).astype(jnp.int32)].add(flat_vals)
    right_side = accumulation[None] * next_adjoint + sources.reshape(K, NX, NY, NZ)

    def one_side(column):
        return solve_one(column, accumulation, tx_eff, ty_eff, tz_eff)

    adjoint_field, residual = lax.map(one_side, right_side)
    return adjoint_field, residual
```

```python
import jax
import jax.numpy as jnp
from jax import lax
from jax.experimental import pallas as pl
from jax.experimental.pallas import tpu as pltpu
from jax.sharding import PartitionSpec as P

F32 = jnp.float32
BF16 = jnp.bfloat16
MESH = pl.DeviceIdType.MESH
K, CX, CY, NZ = 4, 16, 16, 1024
NGX, NGY = 16, 8
PERF, WELLS = 16, 64
RHS = range(K)


def remote(src, dst, send, recv, axis, index):
    return pltpu.make_async_remote_copy(
        src_ref=src, dst_ref=dst, send_sem=send, recv_sem=recv,
        device_id={axis: index}, device_id_type=MESH,
    )


def lanes():
    return lax.broadcasted_iota(jnp.int32, (8, 128), 1)


def rows():
    return lax.broadcasted_iota(jnp.int32, (8, 128), 0)


def column(ref, lead, y):
    return ref[(*lead, pl.ds(8 * y, 8), slice(None))]


def layer_above(ref, lead, y, here, lane):
    nxt = ref[(*lead, pl.ds(8 * y + 1, 8), slice(None))]
    return pltpu.roll(jnp.where(lane == 0, nxt, here), 127, 1)


def layer_below(ref, lead, y, here, lane):
    prv = ref[(*lead, pl.ds(8 * y - 1, 8), slice(None))]
    return pltpu.roll(jnp.where(lane == 127, prv, here), 1, 1)


def main_kernel(
    na_h, acc_h, tx_h, ty_h, tz_h, own_h, site_h, lay_h, cnt_h, wi_h, mis_h,
    b, q, w, sp,
    na, co, src, diag, txc, tyc, tzc, tzm,
    own, site, lay, cnt, wi, mis, packed, out1, in1, out2, in2, left, right, red_out, red1, red2,
    load_sem, well_sem, s1, r1, s2, r2, hs, hr, as1, ar1, as2, ar2,
):
    gx, gy = lax.axis_index("gx"), lax.axis_index("gy")
    up_x, down_x = lax.rem(gx + 1, NGX), lax.rem(gx + NGX - 1, NGX)
    up_y, down_y = lax.rem(gy + 1, NGY), lax.rem(gy + NGY - 1, NGY)

    wells = [pltpu.make_async_copy(h, v, well_sem.at[i]) for i, (h, v) in enumerate(
        ((own_h, own), (site_h, site), (lay_h, lay), (cnt_h, cnt), (wi_h, wi), (mis_h, mis)))]
    for c in wells:
        c.start()
    coef = [pltpu.make_async_copy(h, co.at[i], load_sem.at[i]) for i, h in enumerate((tx_h, ty_h, tz_h, acc_h))]
    for c in coef:
        c.start()
    fields = [pltpu.make_async_copy(na_h.at[k], na.at[k], load_sem.at[4 + k]) for k in RHS]
    for c in fields:
        c.start()

    barrier = pltpu.get_barrier_semaphore()
    for d in range(1, NGY):
        pl.semaphore_signal(barrier, inc=1, device_id={"gy": lax.rem(gy + d, NGY)}, device_id_type=MESH)
    for d in range(1, NGX):
        pl.semaphore_signal(barrier, inc=1, device_id={"gx": lax.rem(gx + d, NGX)}, device_id_type=MESH)

    for c in wells:
        c.wait()
    used = lax.broadcasted_iota(jnp.int32, (PERF, WELLS), 0) < cnt[...]
    packed[...] = jnp.zeros_like(packed)
    packed[0:16, :] = jnp.where(used, wi[...], 0.0)
    packed[16:32, :] = lay[...].astype(F32)
    packed[32:36, :] = mis[...]
    packed[36:37, :] = site[...].astype(F32)
    owner = own[...]
    place = lax.rem(owner, NGY) * NGX + owner // NGY
    onehot = jnp.where(lax.broadcasted_iota(jnp.int32, (128, WELLS), 0) == place, 1.0, 0.0).astype(F32)
    out1[...] = lax.dot_general(
        onehot, packed[...], (((1,), (1,)), ((), ())),
        precision=lax.Precision.HIGHEST, preferred_element_type=F32,
    ).reshape(NGY, NGX, 128)

    pl.semaphore_wait(barrier, NGX + NGY - 2)

    first = []
    for d in range(1, NGY):
        to = lax.rem(gy + d, NGY)
        first.append(remote(out1.at[to], in1.at[pl.ds(gy * NGX, NGX)], s1.at[d], r1.at[d], "gy", to))
    for c in first:
        c.start()
    in1[pl.ds(gy * NGX, NGX), :] = out1[gy]

    last_x = gx == NGX - 1
    last_y = gy == NGY - 1

    def spread(i, put):
        def at(x, _):
            for t in range(2):
                for c in range(8):
                    put(x, t, c, co[i, x, pl.ds(8 * t, 8), pl.ds(128 * c, 128)])
            return 0
        coef[i].wait()
        lax.fori_loop(0, CX, at, 0)

    def put_x(x, t, c, v):
        txc[x + 1, pl.ds(64 * t + c, 8, stride=8), :] = jnp.where(last_x & (x == CX - 1), 0.0, v)

    def put_y(x, t, c, v):
        if t == 1:
            v = jnp.where(last_y & (rows() == 7), 0.0, v)
        tyc[x, pl.ds(8 + 64 * t + c, 8, stride=8), :] = v

    def put_z(x, t, c, v):
        if c == 7:
            v = jnp.where(lanes() == 127, 0.0, v)
        tzc[x, pl.ds(8 + 64 * t + c, 8, stride=8), :] = v

    def put_a(x, t, c, v):
        diag[x, pl.ds(64 * t + c, 8, stride=8), :] = v

    spread(0, put_x)
    face_tx = remote(txc.at[CX], txc.at[0], hs.at[0], hr.at[0], "gx", up_x)
    face_tx.start()
    spread(1, put_y)
    face_ty = remote(tyc.at[:, pl.ds(8 * CY, 8)], tyc.at[:, pl.ds(0, 8)], hs.at[1], hr.at[1], "gy", up_y)
    face_ty.start()

    for c in first:
        c.wait()
    for to in range(NGX):
        out2[to] = in1[pl.ds(to, NGY, stride=NGX), :]
    second = []
    for d in range(1, NGX):
        to = lax.rem(gx + d, NGX)
        second.append(remote(out2.at[to], in2.at[pl.ds(gx * NGY, NGY)], s2.at[d], r2.at[d], "gx", to))
    for c in second:
        c.start()
    in2[pl.ds(gx * NGY, NGY), :] = out2[gx]

    spread(2, put_z)
    spread(3, put_a)
    face_tx.wait()
    face_ty.wait()
    tzc[:, 0:8, :] = jnp.zeros((CX, 8, 128), F32)

    def diagonal(x, _):
        lane = lanes()
        start = (rows() == 0) & (lane == 0)
        ty_low = column(tyc, (x,), 0)
        for y in range(CY):
            here = column(tzc, (x,), y + 1)
            below = jnp.where(start, 0.0, layer_below(tzc, (x,), y + 1, here, lane))
            tzm[x, pl.ds(8 * y, 8), :] = below
            ty_here = column(tyc, (x,), y + 1)
            diag[x, pl.ds(8 * y, 8), :] = (
                column(diag, (x,), y) + (column(txc, (x + 1,), y) + column(txc, (x,), y))
                + (ty_here + ty_low) + (here + below)
            )
            ty_low = ty_here
        return 0

    lax.fori_loop(0, CX, diagonal, 0)

    for c in second:
        c.wait()

    across = in2[...].T

    def split(v):
        high = v.astype(BF16).astype(F32)
        return high, (v - high)

    mis_high, mis_low = split(across[32:36, :])
    spot = lax.broadcasted_iota(jnp.int32, (256, 128), 0).astype(F32) == across[36:37, :]
    for k in RHS:
        high = jnp.where(spot, mis_high[k : k + 1, :], 0.0).astype(BF16)
        left[pl.ds(256 * k, 256), 0:128] = high
        left[pl.ds(256 * k, 256), 128:256] = high
        left[pl.ds(256 * k, 256), 256:384] = jnp.where(spot, mis_low[k : k + 1, :], 0.0).astype(BF16)

    def terms(t, _):
        lane = lanes().astype(F32)
        at = pl.ds(pl.multiple_of(16 * t, 16), 16)
        high, low = [], []
        for half in range(2):
            tile = in2[pl.ds(pl.multiple_of(16 * t + 8 * half, 8), 8), :]
            total = [jnp.zeros((8, 128), F32) for _ in range(8)]
            for p in range(PERF):
                value = jnp.broadcast_to(tile[:, p : p + 1], (8, 128))
                layer = jnp.broadcast_to(tile[:, 16 + p : 17 + p], (8, 128))
                for c in range(8):
                    total[c] = total[c] + jnp.where(layer == lane + 128.0 * c, value, 0.0)
            total = jnp.concatenate(total, axis=1)
            h, l = split(total)
            high.append(h)
            low.append(l)
        high = jnp.concatenate(high, axis=0).astype(BF16)
        right[at, :] = high
        right[pl.ds(pl.multiple_of(128 + 16 * t, 16), 16), :] = jnp.concatenate(low, axis=0).astype(BF16)
        right[pl.ds(pl.multiple_of(256 + 16 * t, 16), 16), :] = high
        return 0

    lax.fori_loop(0, 8, terms, 0)

    def gather(n, _):
        at = pl.ds(pl.multiple_of(256 * n, 256), 256)
        src[:, at] = jnp.dot(left[...], right[:, at], preferred_element_type=F32)
        return 0

    lax.fori_loop(0, 4, gather, 0)

    for c in fields:
        c.wait()

    def begin(x):
        for k in RHS:
            for t in range(2):
                for c in range(8):
                    at = (pl.ds(8 * t, 8), pl.ds(128 * c, 128))
                    v = co[3, x, *at] * na[k, x, *at] + src[
                        pl.ds(pl.multiple_of(256 * k + 16 * x + 8 * t, 8), 8), pl.ds(128 * c, 128)]
                    b[k, x + 1, pl.ds(8 + 64 * t + c, 8, stride=8), :] = v

    def faces_x(f, at):
        body = pl.ds(8, 128)
        return [
            remote(f.at[:, 1, body], f.at[:, CX + 1, body], hs.at[at], hr.at[at], "gx", down_x),
            remote(f.at[:, CX, body], f.at[:, 0, body], hs.at[at + 1], hr.at[at + 1], "gx", up_x),
        ]

    def faces_y(f, at):
        body = pl.ds(1, CX)
        return [
            remote(f.at[:, body, pl.ds(8, 8)], f.at[:, body, pl.ds(8 * CY + 8, 8)], hs.at[at], hr.at[at], "gy", down_y),
            remote(f.at[:, body, pl.ds(8 * CY, 8)], f.at[:, body, pl.ds(0, 8)], hs.at[at + 1], hr.at[at + 1], "gy", up_y),
        ]

    def loop(lo, hi, fn):
        def body(x, _):
            fn(x)
            return 0
        lax.fori_loop(lo, hi, body, 0)

    def apply(v, put, x, ys, sums):
        lane = lanes()
        sums = list(sums)
        prev = None
        for y in ys:
            cols = (x - 1,)
            d = column(diag, cols, y - 1)
            txp, txl = column(txc, (x,), y - 1), column(txc, (x - 1,), y - 1)
            typ = column(tyc, cols, y)
            tzp, tzl = column(tzc, cols, y), column(tzm, cols, y - 1)
            if prev is None or prev[0] != y - 1:
                prev = (y - 1, column(tyc, cols, y - 1), [column(v, (k, x), y - 1) for k in RHS],
                        [column(v, (k, x), y) for k in RHS])
            _, tyl, low, mid = prev
            high = [column(v, (k, x), y + 1) for k in RHS]
            for k in RHS:
                here = mid[k]
                out = (
                    d * here
                    - (txp * column(v, (k, x + 1), y) + txl * column(v, (k, x - 1), y))
                    - (typ * high[k] + tyl * low[k])
                    - (tzp * layer_above(v, (k, x), y, here, lane) + tzl * layer_below(v, (k, x), y, here, lane))
                )
                put(k, x, y, out)
                sums[k] = sums[k] + here * here
                sums[K + k] = sums[K + k] + here * out
            prev = (y, typ, mid, high)
        return tuple(sums)

    def put_q(k, x, y, out):
        q[k, x, pl.ds(8 * y, 8), :] = out

    def put_w(k, x, y, out):
        w[k, x - 1, pl.ds(8 * (y - 1), 8), :] = out

    def inner(v, put, sums):
        return lax.fori_loop(2, CX, lambda x, s: apply(v, put, x, range(2, CY), s), sums)

    def ends(v, put, sums):
        return lax.fori_loop(0, 2, lambda i, s: apply(v, put, 1 + (CX - 1) * i, range(1, CY + 1), s), sums)

    def sides(v, put, sums):
        return lax.fori_loop(2, CX, lambda x, s: apply(v, put, x, (1, CY), s), sums)

    loop(0, 2, lambda i: begin((CX - 1) * i))
    bx = faces_x(b, 2)
    for c in bx:
        c.start()
    loop(1, CX - 1, begin)
    by = faces_y(b, 4)
    for c in by:
        c.start()

    none = tuple(jnp.zeros((8, 128), F32) for _ in range(2 * K))
    one = inner(b, put_q, none)
    for c in by + bx:
        c.wait()
    one = ends(b, put_q, one)
    qx = faces_x(q, 6)
    for c in qx:
        c.start()
    one = sides(b, put_q, one)
    qy = faces_y(q, 8)
    for c in qy:
        c.start()
    two = inner(q, put_w, none)
    for c in qy:
        c.wait()
    two = sides(q, put_w, two)
    for c in qx:
        c.wait()
    two = ends(q, put_w, two)

    lane1 = lax.broadcasted_iota(jnp.int32, (1, 128), 1)
    line = jnp.zeros((1, 128), F32)
    for i, s in enumerate(one + two):
        line = jnp.where(lane1 == i, jnp.sum(s, keepdims=True), line)
    red_out[0] = line
    red1[gx] = line
    hops = []
    for d in range(1, NGX):
        to = lax.rem(gx + d, NGX)
        hops.append(remote(red_out.at[0], red1.at[gx], as1.at[d], ar1.at[d], "gx", to))
    for c in hops:
        c.start()
    for c in hops:
        c.wait()
    line = jnp.sum(red1[...], axis=0)
    red_out[1] = line
    red2[gy] = line
    hops = []
    for d in range(1, NGY):
        to = lax.rem(gy + d, NGY)
        hops.append(remote(red_out.at[1], red2.at[gy], as2.at[d], ar2.at[d], "gy", to))
    for c in hops:
        c.start()
    for c in hops:
        c.wait()
    line = jnp.sum(red2[...], axis=0)

    rr = line
    bq = pltpu.roll(line, 128 - K, 1)
    qq = pltpu.roll(line, 128 - 2 * K, 1)
    qw = pltpu.roll(line, 128 - 3 * K, 1)
    step0 = rr / bq
    rr1 = step0 * step0 * qq - rr
    grow = 1.0 + rr1 / rr
    step1 = rr1 / (grow * grow * bq - 2.0 * grow * step0 * qq + step0 * step0 * qw)
    sp[0] = step0 + step1 * grow
    sp[1] = step0 * step1


def last_kernel(b, q, w, sp, x_h, r_h, xo, ro, sem):
    ones = [jnp.broadcast_to(sp[0][:, k : k + 1], (8, 128)) for k in RHS]
    twos = [jnp.broadcast_to(sp[1][:, k : k + 1], (8, 128)) for k in RHS]
    copies = []
    step = 4

    def at(x, _):
        for k in RHS:
            for t in range(2):
                for c in range(8):
                    bv = b[k, x + 1, pl.ds(8 + 64 * t + c, 8, stride=8), :]
                    qv = q[k, x + 1, pl.ds(8 + 64 * t + c, 8, stride=8), :]
                    wv = w[k, x, pl.ds(64 * t + c, 8, stride=8), :]
                    to = (k, x, pl.ds(8 * t, 8), pl.ds(128 * c, 128))
                    xo[to] = ones[k] * bv - twos[k] * qv
                    ro[to] = bv - ones[k] * qv + twos[k] * wv
        return 0

    for i in range(CX // step):
        lax.fori_loop(i * step, (i + 1) * step, at, 0)
        part = pl.ds(i * step, step)
        for j, (s, h) in enumerate(((xo, x_h), (ro, r_h))):
            c = pltpu.make_async_copy(s.at[:, part], h.at[:, part], sem.at[2 * i + j])
            c.start()
            copies.append(c)
    for c in copies:
        c.wait()


def body(next_adjoint, accumulation, trans_x, trans_y, trans_z,
         well_owner, well_site, perf_layers, perf_count, well_index, misfit):
    dma = pltpu.SemaphoreType.DMA
    vm = pltpu.VMEM
    field = (K, CX + 2, 8 * (CY + 2), 128)
    plane = (CX, 8 * CY, 128)
    anywhere = pl.BlockSpec(memory_space=pl.ANY)
    inside = pl.BlockSpec(memory_space=pltpu.VMEM)
    b, q, w, sp = pl.pallas_call(
        main_kernel,
        out_shape=(
            pltpu.VMEM(field, F32), pltpu.VMEM(field, F32), pltpu.VMEM((K, *plane), F32), pltpu.VMEM((2, 1, 128), F32),
        ),
        in_specs=[anywhere] * 11,
        out_specs=(inside,) * 4,
        scratch_shapes=[
            vm((K, CX, CY, NZ), F32), vm((4, CX, CY, NZ), F32), vm((K * CX * CY, NZ), F32),
            vm(plane, F32), vm((CX + 1, 8 * CY, 128), F32), vm((CX, 8 * CY + 8, 128), F32),
            vm((CX, 8 * CY + 8, 128), F32), vm(plane, F32),
            vm((1, WELLS), jnp.int32), vm((1, WELLS), jnp.int32), vm((PERF, WELLS), jnp.int32),
            vm((1, WELLS), jnp.int32), vm((PERF, WELLS), F32), vm((K, WELLS), F32),
            vm((128, WELLS), F32), vm((NGY, NGX, 128), F32), vm((NGY * NGX, 128), F32),
            vm((NGX, NGY, 128), F32), vm((NGX * NGY, 128), F32),
            vm((K * CX * CY, 384), BF16), vm((384, NZ), BF16),
            vm((2, 1, 128), F32), vm((NGX, 1, 128), F32), vm((NGY, 1, 128), F32),
            dma((8,)), dma((6,)), dma((NGY,)), dma((NGY,)), dma((NGX,)), dma((NGX,)),
            dma((10,)), dma((10,)), dma((NGX,)), dma((NGX,)), dma((NGY,)), dma((NGY,)),
        ],
        compiler_params=pltpu.CompilerParams(
            collective_id=0, has_side_effects=True, vmem_limit_bytes=40 * 2**20),
        cost_estimate=pl.CostEstimate(flops=60_000_000, bytes_accessed=9_000_000, transcendentals=0),
        name="adjoint_krylov",
    )(next_adjoint, accumulation, trans_x, trans_y, trans_z, well_owner.T, well_site.reshape(1, WELLS),
      perf_layers.T, perf_count.reshape(1, WELLS), well_index.T, misfit.T)
    out = jax.ShapeDtypeStruct((K, CX, CY, NZ), F32)
    return pl.pallas_call(
        last_kernel,
        out_shape=(out, out),
        in_specs=[inside] * 4,
        out_specs=(anywhere, anywhere),
        scratch_shapes=[vm((K, CX, CY, NZ), F32), vm((K, CX, CY, NZ), F32), dma((8,))],
        compiler_params=pltpu.CompilerParams(vmem_limit_bytes=24 * 2**20),
        name="adjoint_result",
    )(b, q, w, sp)


def solution(mesh):
    flat = P(("gx", "gy"))
    rows_of = P(("gx", "gy"), None)
    cells = P("gx", "gy", None)
    many = P(None, "gx", "gy", None)
    return jax.shard_map(
        body,
        mesh=mesh,
        in_specs=(many, cells, cells, cells, cells, rows_of, flat, rows_of, flat, rows_of, rows_of),
        out_specs=(many, many),
        check_vma=False,
    )
```

```python
import jax
import jax.numpy as jnp
from jax import lax
from jax.experimental import pallas as pl
from jax.experimental.pallas import tpu as pltpu
from jax.sharding import PartitionSpec as P

F32 = jnp.float32
BF16 = jnp.bfloat16
MESH = pl.DeviceIdType.MESH
K, CX, CY, NZ = 4, 16, 16, 1024
NGX, NGY = 16, 8
PERF, WELLS = 16, 64
RHS = range(K)


def remote(src, dst, send, recv, axis, index):
    return pltpu.make_async_remote_copy(
        src_ref=src, dst_ref=dst, send_sem=send, recv_sem=recv,
        device_id={axis: index}, device_id_type=MESH,
    )


def lanes():
    return lax.broadcasted_iota(jnp.int32, (8, 128), 1)


def rows():
    return lax.broadcasted_iota(jnp.int32, (8, 128), 0)


def column(ref, lead, y):
    return ref[(*lead, pl.ds(8 * y, 8), slice(None))]


def layer_above(ref, lead, y, here, lane):
    nxt = pltpu.roll(here, 7, 0) if y == CY else ref[(*lead, pl.ds(8 * y + 1, 8), slice(None))]
    return pltpu.roll(jnp.where(lane == 0, nxt, here), 127, 1)


def layer_below(ref, lead, y, here, lane):
    prv = pltpu.roll(here, 1, 0) if y == 1 else ref[(*lead, pl.ds(8 * y - 1, 8), slice(None))]
    return pltpu.roll(jnp.where(lane == 127, prv, here), 1, 1)


def main_kernel(
    na_h, acc_h, tx_h, ty_h, tz_h, own_h, site_h, lay_h, cnt_h, wi_h, mis_h,
    b, q, w, sp,
    na, co, src, diag, txc, tyc, tzc, tzm,
    own, site, lay, cnt, wi, mis, packed, out1, in1, out2, in2, left, right, send_x, send_y, red_out, red1, red2,
    load_sem, well_sem, s1, r1, s2, r2, hs, hr, as1, ar1, as2, ar2,
):
    gx, gy = lax.axis_index("gx"), lax.axis_index("gy")
    up_x, down_x = lax.rem(gx + 1, NGX), lax.rem(gx + NGX - 1, NGX)
    up_y, down_y = lax.rem(gy + 1, NGY), lax.rem(gy + NGY - 1, NGY)

    wells = [pltpu.make_async_copy(h, v, well_sem.at[i]) for i, (h, v) in enumerate(
        ((own_h, own), (site_h, site), (lay_h, lay), (cnt_h, cnt), (wi_h, wi), (mis_h, mis)))]
    for c in wells:
        c.start()
    coef = [pltpu.make_async_copy(h, co.at[i], load_sem.at[i]) for i, h in enumerate((tx_h, ty_h, tz_h, acc_h))]
    for c in coef:
        c.start()
    fields = [pltpu.make_async_copy(na_h.at[k], na.at[k], load_sem.at[4 + k]) for k in RHS]
    for c in fields:
        c.start()

    barrier = pltpu.get_barrier_semaphore()
    for d in range(1, NGY):
        pl.semaphore_signal(barrier, inc=1, device_id={"gy": lax.rem(gy + d, NGY)}, device_id_type=MESH)
    for d in range(1, NGX):
        pl.semaphore_signal(barrier, inc=1, device_id={"gx": lax.rem(gx + d, NGX)}, device_id_type=MESH)

    for c in wells:
        c.wait()
    used = lax.broadcasted_iota(jnp.int32, (PERF, WELLS), 0) < cnt[...]
    packed[...] = jnp.zeros_like(packed)
    packed[0:16, :] = jnp.where(used, wi[...], 0.0)
    packed[16:32, :] = lay[...].astype(F32)
    packed[32:36, :] = mis[...]
    packed[36:37, :] = site[...].astype(F32)
    owner = own[...]
    place = lax.rem(owner, NGY) * NGX + owner // NGY
    onehot = jnp.where(lax.broadcasted_iota(jnp.int32, (128, WELLS), 0) == place, 1.0, 0.0).astype(F32)
    out1[...] = lax.dot_general(
        onehot, packed[...], (((1,), (1,)), ((), ())),
        precision=lax.Precision.HIGHEST, preferred_element_type=F32,
    ).reshape(NGY, NGX, 128)

    pl.semaphore_wait(barrier, NGX + NGY - 2)

    first = []
    for d in range(1, NGY):
        to = lax.rem(gy + d, NGY)
        first.append(remote(out1.at[to], in1.at[pl.ds(gy * NGX, NGX)], s1.at[d], r1.at[d], "gy", to))
    for c in first:
        c.start()
    in1[pl.ds(gy * NGX, NGX), :] = out1[gy]

    last_x = gx == NGX - 1
    last_y = gy == NGY - 1

    def spread(i, put):
        def at(x, _):
            for t in range(2):
                for c in range(8):
                    put(x, t, c, co[i, x, pl.ds(8 * t, 8), pl.ds(128 * c, 128)])
            return 0
        coef[i].wait()
        lax.fori_loop(0, CX, at, 0)

    def put_x(x, t, c, v):
        txc[x + 1, pl.ds(64 * t + c, 8, stride=8), :] = jnp.where(last_x & (x == CX - 1), 0.0, v)

    def put_y(x, t, c, v):
        if t == 1:
            v = jnp.where(last_y & (rows() == 7), 0.0, v)
        tyc[x, pl.ds(8 + 64 * t + c, 8, stride=8), :] = v

    def put_z(x, t, c, v):
        if c == 7:
            v = jnp.where(lanes() == 127, 0.0, v)
        tzc[x, pl.ds(8 + 64 * t + c, 8, stride=8), :] = v

    def put_a(x, t, c, v):
        diag[x, pl.ds(64 * t + c, 8, stride=8), :] = v

    spread(0, put_x)
    face_tx = remote(txc.at[CX], txc.at[0], hs.at[0], hr.at[0], "gx", up_x)
    face_tx.start()
    spread(1, put_y)
    face_ty = remote(tyc.at[:, pl.ds(8 * CY, 8)], tyc.at[:, pl.ds(0, 8)], hs.at[1], hr.at[1], "gy", up_y)
    face_ty.start()

    for c in first:
        c.wait()
    for to in range(NGX):
        out2[to] = in1[pl.ds(to, NGY, stride=NGX), :]
    second = []
    for d in range(1, NGX):
        to = lax.rem(gx + d, NGX)
        second.append(remote(out2.at[to], in2.at[pl.ds(gx * NGY, NGY)], s2.at[d], r2.at[d], "gx", to))
    for c in second:
        c.start()
    in2[pl.ds(gx * NGY, NGY), :] = out2[gx]

    spread(2, put_z)
    spread(3, put_a)
    face_tx.wait()
    face_ty.wait()
    tzc[:, 0:8, :] = jnp.zeros((CX, 8, 128), F32)

    def diagonal(x, _):
        lane = lanes()
        start = (rows() == 0) & (lane == 0)
        ty_low = column(tyc, (x,), 0)
        for y in range(CY):
            here = column(tzc, (x,), y + 1)
            below = jnp.where(start, 0.0, layer_below(tzc, (x,), y + 1, here, lane))
            tzm[x, pl.ds(8 * y, 8), :] = below
            ty_here = column(tyc, (x,), y + 1)
            diag[x, pl.ds(8 * y, 8), :] = (
                column(diag, (x,), y) + (column(txc, (x + 1,), y) + column(txc, (x,), y))
                + (ty_here + ty_low) + (here + below)
            )
            ty_low = ty_here
        return 0

    lax.fori_loop(0, CX, diagonal, 0)

    for c in second:
        c.wait()

    def block(x):
        if isinstance(x, int):
            return K * CY * (0 if x == 0 else 1 if x == CX - 1 else x + 1)
        return pl.multiple_of(K * CY * (x + 1), K * CY)

    across = in2[...].T

    def split(v):
        high = v.astype(BF16).astype(F32)
        return high, (v - high)

    mis_high, mis_low = split(across[32:36, :])
    for x in range(CX):
        spot = (lax.broadcasted_iota(jnp.int32, (CY, 128), 0) + CY * x).astype(F32) == across[36:37, :]
        for k in RHS:
            at = pl.ds(block(x) + CY * k, CY)
            high = jnp.where(spot, mis_high[k : k + 1, :], 0.0).astype(BF16)
            left[at, 0:128] = high
            left[at, 128:256] = high
            left[at, 256:384] = jnp.where(spot, mis_low[k : k + 1, :], 0.0).astype(BF16)

    def terms(t, _):
        lane = lanes().astype(F32)
        at = pl.ds(pl.multiple_of(16 * t, 16), 16)
        high, low = [], []
        for half in range(2):
            tile = in2[pl.ds(pl.multiple_of(16 * t + 8 * half, 8), 8), :]
            total = [jnp.zeros((8, 128), F32) for _ in range(8)]
            for p in range(PERF):
                value = jnp.broadcast_to(tile[:, p : p + 1], (8, 128))
                layer = jnp.broadcast_to(tile[:, 16 + p : 17 + p], (8, 128))
                for c in range(8):
                    total[c] = total[c] + jnp.where(layer == lane + 128.0 * c, value, 0.0)
            total = jnp.concatenate(total, axis=1)
            h, l = split(total)
            high.append(h)
            low.append(l)
        high = jnp.concatenate(high, axis=0).astype(BF16)
        right[at, :] = high
        right[pl.ds(pl.multiple_of(128 + 16 * t, 16), 16), :] = jnp.concatenate(low, axis=0).astype(BF16)
        right[pl.ds(pl.multiple_of(256 + 16 * t, 16), 16), :] = high
        return 0

    lax.fori_loop(0, 8, terms, 0)

    def gather(part):
        def at(n, _):
            here = pl.ds(pl.multiple_of(256 * n, 256), 256)
            src[part, here] = jnp.dot(left[part, :], right[:, here], preferred_element_type=F32)
            return 0
        lax.fori_loop(0, NZ // 256, at, 0)

    for c in fields:
        c.wait()

    def begin(x):
        for k in RHS:
            for t in range(2):
                for c in range(8):
                    at = (pl.ds(8 * t, 8), pl.ds(128 * c, 128))
                    row = block(x) + (CY * k + 8 * t)
                    row = row if isinstance(x, int) else pl.multiple_of(row, 8)
                    v = co[3, x, *at] * na[k, x, *at] + src[pl.ds(row, 8), pl.ds(128 * c, 128)]
                    b[k, x + 1, pl.ds(8 + 64 * t + c, 8, stride=8), :] = v

    def face(src_ref, dst_ref, at, axis, to):
        return remote(src_ref, dst_ref, hs.at[at], hr.at[at], axis, to)

    low, high = pl.ds(8, 8), pl.ds(8 * CY, 8)
    before, after = pl.ds(0, 8), pl.ds(8 * CY + 8, 8)

    def loop(lo, hi, fn):
        def body(x, _):
            fn(x)
            return 0
        lax.fori_loop(lo, hi, body, 0)

    def apply(v, put, x, ys, sums, halo=True, dots=True):
        lane = lanes()
        sums = list(sums)
        prev = None
        for y in ys:
            cols = (x - 1,)
            d = column(diag, cols, y - 1)
            txp, txl = column(txc, (x,), y - 1), column(txc, (x - 1,), y - 1)
            typ = column(tyc, cols, y)
            tzp, tzl = column(tzc, cols, y), column(tzm, cols, y - 1)
            if prev is None or prev[0] != y - 1:
                prev = (y - 1, column(tyc, cols, y - 1), [column(v, (k, x), y - 1) if halo or y > 1 else None for k in RHS],
                        [column(v, (k, x), y) for k in RHS])
            _, tyl, down, mid = prev
            up = [column(v, (k, x), y + 1) if halo or y < CY else None for k in RHS]
            for k in RHS:
                here = mid[k]
                out = d * here
                if halo or not (isinstance(x, int) and x == CX):
                    out = out - txp * column(v, (k, x + 1), y)
                if halo or not (isinstance(x, int) and x == 1):
                    out = out - txl * column(v, (k, x - 1), y)
                if up[k] is not None:
                    out = out - typ * up[k]
                if down[k] is not None:
                    out = out - tyl * down[k]
                out = out - (tzp * layer_above(v, (k, x), y, here, lane) + tzl * layer_below(v, (k, x), y, here, lane))
                put(k, x, y, out)
                if dots:
                    sums[k] = sums[k] + here * here
                    sums[K + k] = sums[K + k] + here * out
            prev = (y, typ, mid, up)
        return tuple(sums)

    def put_q(k, x, y, out):
        q[k, x, pl.ds(8 * y, 8), :] = out

    def put_end(k, x, y, out):
        put_q(k, x, y, out)
        send_x[0 if x == 1 else 1, k, pl.ds(8 * (y - 1), 8), :] = out

    def put_side(k, x, y, out):
        put_q(k, x, y, out)
        send_y[0 if y == 1 else 1, k, x - 1] = out

    def put_w(k, x, y, out):
        w[k, x - 1, pl.ds(8 * (y - 1), 8), :] = out

    def inner(v, put, sums):
        return lax.fori_loop(2, CX, lambda x, s: apply(v, put, x, range(2, CY), s), sums)

    def ends(v, put, sums, **kw):
        for x in (1, CX):
            sums = apply(v, put, x, range(1, CY + 1), sums, **kw)
        return sums

    def sides(v, put, sums, **kw):
        def at(i, s):
            for j in range(7):
                s = apply(v, put, 2 + 7 * i + j, (1, CY), s, **kw)
            return s
        return lax.fori_loop(0, 2, at, sums)

    none = tuple(jnp.zeros((8, 128), F32) for _ in range(2 * K))
    planes = pl.ds(8, 8 * CY)
    inside_y = pl.ds(16, 8 * (CY - 2))
    inside_x = pl.ds(2, CX - 2)
    all_x = pl.ds(1, CX)

    gather(pl.ds(0, 2 * K * CY))
    begin(0)
    begin(CX - 1)
    bx = [face(b.at[:, 1, planes], b.at[:, CX + 1, planes], 2, "gx", down_x),
          face(b.at[:, CX, planes], b.at[:, 0, planes], 3, "gx", up_x)]
    for c in bx:
        c.start()
    gather(pl.ds(2 * K * CY, (CX - 2) * K * CY))
    loop(1, CX - 1, begin)
    by = [face(b.at[:, all_x, low], b.at[:, all_x, after], 4, "gy", down_y),
          face(b.at[:, all_x, high], b.at[:, all_x, before], 5, "gy", up_y)]
    for c in by:
        c.start()

    ends(b, put_end, none, halo=False, dots=False)
    inner_rows = pl.ds(8, 8 * (CY - 2))
    qx = [face(send_x.at[0, :, inner_rows], q.at[:, CX + 1, inside_y], 6, "gx", down_x),
          face(send_x.at[1, :, inner_rows], q.at[:, 0, inside_y], 7, "gx", up_x)]
    for c in qx:
        c.start()
    sides(b, put_side, none, halo=False, dots=False)
    inner_planes = pl.ds(1, CX - 2)
    qy = [face(send_y.at[0, :, inner_planes], q.at[:, inside_x, after], 8, "gy", down_y),
          face(send_y.at[1, :, inner_planes], q.at[:, inside_x, before], 9, "gy", up_y)]
    for c in qy:
        c.start()
    one = inner(b, put_q, none)

    def complete(x, y, sums):
        sums = list(sums)
        for k in RHS:
            here = column(b, (k, x), y)
            out = column(q, (k, x), y)
            if isinstance(x, int):
                edge = 0 if x == 1 else CX
                out = out - column(txc, (edge,), y - 1) * column(b, (k, 0 if x == 1 else CX + 1), y)
            if y == 1:
                out = out - column(tyc, (x - 1,), 0) * column(b, (k, x), 0)
            if y == CY:
                out = out - column(tyc, (x - 1,), CY) * column(b, (k, x), CY + 1)
            put_q(k, x, y, out)
            sums[k] = sums[k] + here * here
            sums[K + k] = sums[K + k] + here * out
        return tuple(sums)

    for c in by + bx:
        c.wait()
    for x in (1, CX):
        for y in (1, CY):
            one = complete(x, y, one)
    corners = []
    for i, (x, to_x, x_axis) in enumerate(((1, CX + 1, down_x), (CX, 0, up_x))):
        for j, (y, to_y, y_axis) in enumerate(((low, after, down_y), (high, before, up_y))):
            at = 10 + 4 * i + 2 * j
            corners.append(face(q.at[:, x, y], q.at[:, to_x, y], at, "gx", x_axis))
            corners.append(face(q.at[:, x, y], q.at[:, x, to_y], at + 1, "gy", y_axis))
    for c in corners:
        c.start()
    for x in (1, CX):
        for y in range(2, CY):
            one = complete(x, y, one)
    one = lax.fori_loop(2, CX, lambda x, s: complete(x, CY, complete(x, 1, s)), one)

    two = inner(q, put_w, none)

    def add(k, x, y, t, v):
        put_q(k, x, y, column(q, (k, x), y) - t * v)

    for c in qy:
        c.wait()

    def beside(x, _):
        for k in RHS:
            add(k, x, 0, column(tyc, (x - 1,), 0), column(b, (k, x), 1))
            add(k, x, CY + 1, column(tyc, (x - 1,), CY), column(b, (k, x), CY))
        return 0

    lax.fori_loop(2, CX, beside, 0)
    two = sides(q, put_w, two)
    for c in qx + corners:
        c.wait()
    for y in range(2, CY):
        for k in RHS:
            add(k, 0, y, column(txc, (0,), y - 1), column(b, (k, 1), y))
            add(k, CX + 1, y, column(txc, (CX,), y - 1), column(b, (k, CX), y))
    two = ends(q, put_w, two)

    lane1 = lax.broadcasted_iota(jnp.int32, (1, 128), 1)
    line = jnp.zeros((1, 128), F32)
    for i, s in enumerate(one + two):
        line = jnp.where(lane1 == i, jnp.sum(s, keepdims=True), line)
    red_out[0] = line
    red1[gx] = line
    hops = []
    for d in range(1, NGX):
        to = lax.rem(gx + d, NGX)
        hops.append(remote(red_out.at[0], red1.at[gx], as1.at[d], ar1.at[d], "gx", to))
    for c in hops:
        c.start()
    for c in hops:
        c.wait()
    line = jnp.sum(red1[...], axis=0)
    red_out[1] = line
    red2[gy] = line
    hops = []
    for d in range(1, NGY):
        to = lax.rem(gy + d, NGY)
        hops.append(remote(red_out.at[1], red2.at[gy], as2.at[d], ar2.at[d], "gy", to))
    for c in hops:
        c.start()
    for c in hops:
        c.wait()
    line = jnp.sum(red2[...], axis=0)

    rr = line
    bq = pltpu.roll(line, 128 - K, 1)
    qq = pltpu.roll(line, 128 - 2 * K, 1)
    qw = pltpu.roll(line, 128 - 3 * K, 1)
    step0 = rr / bq
    rr1 = step0 * step0 * qq - rr
    grow = 1.0 + rr1 / rr
    step1 = rr1 / (grow * grow * bq - 2.0 * grow * step0 * qq + step0 * step0 * qw)
    sp[0] = step0 + step1 * grow
    sp[1] = step0 * step1


def last_kernel(b, q, w, sp, x_h, r_h, xo, ro, sem):
    ones = [jnp.broadcast_to(sp[0][:, k : k + 1], (8, 128)) for k in RHS]
    twos = [jnp.broadcast_to(sp[1][:, k : k + 1], (8, 128)) for k in RHS]
    copies = []
    step = 2

    def at(x, _):
        for k in RHS:
            for t in range(2):
                for c in range(8):
                    bv = b[k, x + 1, pl.ds(8 + 64 * t + c, 8, stride=8), :]
                    qv = q[k, x + 1, pl.ds(8 + 64 * t + c, 8, stride=8), :]
                    wv = w[k, x, pl.ds(64 * t + c, 8, stride=8), :]
                    to = (k, x, pl.ds(8 * t, 8), pl.ds(128 * c, 128))
                    xo[to] = ones[k] * bv - twos[k] * qv
                    ro[to] = bv - ones[k] * qv + twos[k] * wv
        return 0

    for i in range(CX // step):
        lax.fori_loop(i * step, (i + 1) * step, at, 0)
        part = pl.ds(i * step, step)
        for j, (s, h) in enumerate(((xo, x_h), (ro, r_h))):
            c = pltpu.make_async_copy(s.at[:, part], h.at[:, part], sem.at[2 * i + j])
            c.start()
            copies.append(c)
    for c in copies:
        c.wait()


def body(next_adjoint, accumulation, trans_x, trans_y, trans_z,
         well_owner, well_site, perf_layers, perf_count, well_index, misfit):
    dma = pltpu.SemaphoreType.DMA
    vm = pltpu.VMEM
    field = (K, CX + 2, 8 * (CY + 2), 128)
    plane = (CX, 8 * CY, 128)
    anywhere = pl.BlockSpec(memory_space=pl.ANY)
    inside = pl.BlockSpec(memory_space=pltpu.VMEM)
    b, q, w, sp = pl.pallas_call(
        main_kernel,
        out_shape=(
            pltpu.VMEM(field, F32), pltpu.VMEM(field, F32), pltpu.VMEM((K, *plane), F32), pltpu.VMEM((2, 1, 128), F32),
        ),
        in_specs=[anywhere] * 11,
        out_specs=(inside,) * 4,
        scratch_shapes=[
            vm((K, CX, CY, NZ), F32), vm((4, CX, CY, NZ), F32), vm((K * CX * CY, NZ), F32),
            vm(plane, F32), vm((CX + 1, 8 * CY, 128), F32), vm((CX, 8 * CY + 8, 128), F32),
            vm((CX, 8 * CY + 8, 128), F32), vm(plane, F32),
            vm((1, WELLS), jnp.int32), vm((1, WELLS), jnp.int32), vm((PERF, WELLS), jnp.int32),
            vm((1, WELLS), jnp.int32), vm((PERF, WELLS), F32), vm((K, WELLS), F32),
            vm((128, WELLS), F32), vm((NGY, NGX, 128), F32), vm((NGY * NGX, 128), F32),
            vm((NGX, NGY, 128), F32), vm((NGX * NGY, 128), F32),
            vm((K * CX * CY, 384), BF16), vm((384, NZ), BF16),
            vm((2, K, 8 * CY, 128), F32), vm((2, K, CX, 8, 128), F32),
            vm((2, 1, 128), F32), vm((NGX, 1, 128), F32), vm((NGY, 1, 128), F32),
            dma((8,)), dma((6,)), dma((NGY,)), dma((NGY,)), dma((NGX,)), dma((NGX,)),
            dma((18,)), dma((18,)), dma((NGX,)), dma((NGX,)), dma((NGY,)), dma((NGY,)),
        ],
        compiler_params=pltpu.CompilerParams(
            collective_id=0, has_side_effects=True, vmem_limit_bytes=40 * 2**20),
        cost_estimate=pl.CostEstimate(flops=60_000_000, bytes_accessed=9_000_000, transcendentals=0),
        name="adjoint_krylov",
    )(next_adjoint, accumulation, trans_x, trans_y, trans_z, well_owner.T, well_site.reshape(1, WELLS),
      perf_layers.T, perf_count.reshape(1, WELLS), well_index.T, misfit.T)
    out = jax.ShapeDtypeStruct((K, CX, CY, NZ), F32)
    return pl.pallas_call(
        last_kernel,
        out_shape=(out, out),
        in_specs=[inside] * 4,
        out_specs=(anywhere, anywhere),
        scratch_shapes=[vm((K, CX, CY, NZ), F32), vm((K, CX, CY, NZ), F32), dma((16,))],
        compiler_params=pltpu.CompilerParams(vmem_limit_bytes=24 * 2**20),
        name="adjoint_result",
    )(b, q, w, sp)


def solution(mesh):
    flat = P(("gx", "gy"))
    rows_of = P(("gx", "gy"), None)
    cells = P("gx", "gy", None)
    many = P(None, "gx", "gy", None)
    return jax.shard_map(
        body,
        mesh=mesh,
        in_specs=(many, cells, cells, cells, cells, rows_of, flat, rows_of, flat, rows_of, rows_of),
        out_specs=(many, many),
        check_vma=False,
    )
```

```python
import jax
import jax.numpy as jnp
from jax import lax
from jax.experimental import pallas as pl
from jax.experimental.pallas import tpu as pltpu
from jax.sharding import PartitionSpec as P

F32 = jnp.float32
BF16 = jnp.bfloat16
MESH = pl.DeviceIdType.MESH
K, CX, CY, NZ = 4, 16, 16, 1024
NGX, NGY = 16, 8
PERF, WELLS = 16, 64
RHS = range(K)


def remote(src, dst, send, recv, axis, index):
    return pltpu.make_async_remote_copy(
        src_ref=src, dst_ref=dst, send_sem=send, recv_sem=recv,
        device_id={axis: index}, device_id_type=MESH,
    )


def lanes():
    return lax.broadcasted_iota(jnp.int32, (8, 128), 1)


def rows():
    return lax.broadcasted_iota(jnp.int32, (8, 128), 0)


def column(ref, lead, y):
    return ref[(*lead, pl.ds(8 * y, 8), slice(None))]


def layer_above(ref, lead, y, here, lane):
    nxt = pltpu.roll(here, 7, 0) if y == CY else ref[(*lead, pl.ds(8 * y + 1, 8), slice(None))]
    return pltpu.roll(jnp.where(lane == 0, nxt, here), 127, 1)


def layer_below(ref, lead, y, here, lane):
    prv = pltpu.roll(here, 1, 0) if y == 1 else ref[(*lead, pl.ds(8 * y - 1, 8), slice(None))]
    return pltpu.roll(jnp.where(lane == 127, prv, here), 1, 1)


def main_kernel(
    na_h, acc_h, tx_h, ty_h, tz_h, own_h, site_h, lay_h, cnt_h, wi_h, mis_h,
    b, q, w, sp,
    na, co, src, diag, txc, tyc, tzc, tzm,
    own, site, lay, cnt, wi, mis, packed, out1, in1, out2, in2, left, right, send_x, send_y, red_out, red1, red2,
    load_sem, well_sem, s1, r1, s2, r2, hs, hr, as1, ar1, as2, ar2,
):
    gx, gy = lax.axis_index("gx"), lax.axis_index("gy")
    up_x, down_x = lax.rem(gx + 1, NGX), lax.rem(gx + NGX - 1, NGX)
    up_y, down_y = lax.rem(gy + 1, NGY), lax.rem(gy + NGY - 1, NGY)

    wells = [pltpu.make_async_copy(h, v, well_sem.at[i]) for i, (h, v) in enumerate(
        ((own_h, own), (site_h, site), (lay_h, lay), (cnt_h, cnt), (wi_h, wi), (mis_h, mis)))]
    for c in wells:
        c.start()
    barrier = pltpu.get_barrier_semaphore()
    for d in range(1, NGY):
        pl.semaphore_signal(barrier, inc=1, device_id={"gy": lax.rem(gy + d, NGY)}, device_id_type=MESH)
    for d in range(1, NGX):
        pl.semaphore_signal(barrier, inc=1, device_id={"gx": lax.rem(gx + d, NGX)}, device_id_type=MESH)

    for c in wells:
        c.wait()
    used = lax.broadcasted_iota(jnp.int32, (PERF, WELLS), 0) < cnt[...]
    packed[...] = jnp.zeros_like(packed)
    packed[0:16, :] = jnp.where(used, wi[...], 0.0)
    packed[16:32, :] = lay[...].astype(F32)
    packed[32:36, :] = mis[...]
    packed[36:37, :] = site[...].astype(F32)
    owner = own[...]
    place = lax.rem(owner, NGY) * NGX + owner // NGY
    onehot = jnp.where(lax.broadcasted_iota(jnp.int32, (128, WELLS), 0) == place, 1.0, 0.0).astype(F32)
    out1[...] = lax.dot_general(
        onehot, packed[...], (((1,), (1,)), ((), ())),
        precision=lax.Precision.HIGHEST, preferred_element_type=F32,
    ).reshape(NGY, NGX, 128)

    pl.semaphore_wait(barrier, NGX + NGY - 2)

    first = []
    for d in range(1, NGY):
        to = lax.rem(gy + d, NGY)
        first.append(remote(out1.at[to], in1.at[pl.ds(gy * NGX, NGX)], s1.at[d], r1.at[d], "gy", to))
    for c in first:
        c.start()
    coef = [pltpu.make_async_copy(h, co.at[i], load_sem.at[i]) for i, h in enumerate((tx_h, ty_h, tz_h, acc_h))]
    for c in coef:
        c.start()
    fields = [pltpu.make_async_copy(na_h.at[k], na.at[k], load_sem.at[4 + k]) for k in RHS]
    for c in fields:
        c.start()

    in1[pl.ds(gy * NGX, NGX), :] = out1[gy]

    last_x = gx == NGX - 1
    last_y = gy == NGY - 1

    def spread(i, put):
        def at(x, _):
            for t in range(2):
                for c in range(8):
                    put(x, t, c, co[i, x, pl.ds(8 * t, 8), pl.ds(128 * c, 128)])
            return 0
        coef[i].wait()
        lax.fori_loop(0, CX, at, 0)

    def put_x(x, t, c, v):
        txc[x + 1, pl.ds(64 * t + c, 8, stride=8), :] = jnp.where(last_x & (x == CX - 1), 0.0, v)

    def put_y(x, t, c, v):
        if t == 1:
            v = jnp.where(last_y & (rows() == 7), 0.0, v)
        tyc[x, pl.ds(8 + 64 * t + c, 8, stride=8), :] = v

    def put_z(x, t, c, v):
        if c == 7:
            v = jnp.where(lanes() == 127, 0.0, v)
        tzc[x, pl.ds(8 + 64 * t + c, 8, stride=8), :] = v

    def put_a(x, t, c, v):
        diag[x, pl.ds(64 * t + c, 8, stride=8), :] = v

    spread(0, put_x)
    face_tx = remote(txc.at[CX], txc.at[0], hs.at[0], hr.at[0], "gx", up_x)
    face_tx.start()
    spread(1, put_y)
    face_ty = remote(tyc.at[:, pl.ds(8 * CY, 8)], tyc.at[:, pl.ds(0, 8)], hs.at[1], hr.at[1], "gy", up_y)
    face_ty.start()

    for c in first:
        c.wait()
    for to in range(NGX):
        out2[to] = in1[pl.ds(to, NGY, stride=NGX), :]
    second = []
    for d in range(1, NGX):
        to = lax.rem(gx + d, NGX)
        second.append(remote(out2.at[to], in2.at[pl.ds(gx * NGY, NGY)], s2.at[d], r2.at[d], "gx", to))
    for c in second:
        c.start()
    in2[pl.ds(gx * NGY, NGY), :] = out2[gx]

    spread(2, put_z)
    spread(3, put_a)
    face_tx.wait()
    face_ty.wait()
    tzc[:, 0:8, :] = jnp.zeros((CX, 8, 128), F32)

    def diagonal(x, _):
        lane = lanes()
        start = (rows() == 0) & (lane == 0)
        ty_low = column(tyc, (x,), 0)
        for y in range(CY):
            here = column(tzc, (x,), y + 1)
            below = jnp.where(start, 0.0, layer_below(tzc, (x,), y + 1, here, lane))
            tzm[x, pl.ds(8 * y, 8), :] = below
            ty_here = column(tyc, (x,), y + 1)
            diag[x, pl.ds(8 * y, 8), :] = (
                column(diag, (x,), y) + (column(txc, (x + 1,), y) + column(txc, (x,), y))
                + (ty_here + ty_low) + (here + below)
            )
            ty_low = ty_here
        return 0

    lax.fori_loop(0, CX, diagonal, 0)

    for c in second:
        c.wait()

    def block(x):
        if isinstance(x, int):
            return K * CY * (0 if x == 0 else 1 if x == CX - 1 else x + 1)
        return pl.multiple_of(K * CY * (x + 1), K * CY)

    across = in2[...].T

    def split(v):
        high = v.astype(BF16).astype(F32)
        return high, (v - high)

    mis_high, mis_low = split(across[32:36, :])
    for x in range(CX):
        spot = (lax.broadcasted_iota(jnp.int32, (CY, 128), 0) + CY * x).astype(F32) == across[36:37, :]
        for k in RHS:
            at = pl.ds(block(x) + CY * k, CY)
            high = jnp.where(spot, mis_high[k : k + 1, :], 0.0).astype(BF16)
            left[at, 0:128] = high
            left[at, 128:256] = high
            left[at, 256:384] = jnp.where(spot, mis_low[k : k + 1, :], 0.0).astype(BF16)

    def terms(t, _):
        lane = lanes().astype(F32)
        at = pl.ds(pl.multiple_of(16 * t, 16), 16)
        high, low = [], []
        for half in range(2):
            tile = in2[pl.ds(pl.multiple_of(16 * t + 8 * half, 8), 8), :]
            total = [jnp.zeros((8, 128), F32) for _ in range(8)]
            for p in range(PERF):
                value = jnp.broadcast_to(tile[:, p : p + 1], (8, 128))
                layer = jnp.broadcast_to(tile[:, 16 + p : 17 + p], (8, 128))
                for c in range(8):
                    total[c] = total[c] + jnp.where(layer == lane + 128.0 * c, value, 0.0)
            total = jnp.concatenate(total, axis=1)
            h, l = split(total)
            high.append(h)
            low.append(l)
        high = jnp.concatenate(high, axis=0).astype(BF16)
        right[at, :] = high
        right[pl.ds(pl.multiple_of(128 + 16 * t, 16), 16), :] = jnp.concatenate(low, axis=0).astype(BF16)
        right[pl.ds(pl.multiple_of(256 + 16 * t, 16), 16), :] = high
        return 0

    lax.fori_loop(0, 8, terms, 0)

    def gather(part):
        def at(n, _):
            here = pl.ds(pl.multiple_of(256 * n, 256), 256)
            src[part, here] = jnp.dot(left[part, :], right[:, here], preferred_element_type=F32)
            return 0
        lax.fori_loop(0, NZ // 256, at, 0)

    for c in fields:
        c.wait()

    def begin(x):
        for k in RHS:
            for t in range(2):
                for c in range(8):
                    at = (pl.ds(8 * t, 8), pl.ds(128 * c, 128))
                    row = block(x) + (CY * k + 8 * t)
                    row = row if isinstance(x, int) else pl.multiple_of(row, 8)
                    v = co[3, x, *at] * na[k, x, *at] + src[pl.ds(row, 8), pl.ds(128 * c, 128)]
                    b[k, x + 1, pl.ds(8 + 64 * t + c, 8, stride=8), :] = v

    def face(src_ref, dst_ref, at, axis, to):
        return remote(src_ref, dst_ref, hs.at[at], hr.at[at], axis, to)

    low, high = pl.ds(8, 8), pl.ds(8 * CY, 8)
    before, after = pl.ds(0, 8), pl.ds(8 * CY + 8, 8)

    def loop(lo, hi, fn):
        def body(x, _):
            fn(x)
            return 0
        lax.fori_loop(lo, hi, body, 0)

    def apply(v, put, x, ys, sums, halo=True, dots=True):
        lane = lanes()
        sums = list(sums)
        prev = None
        for y in ys:
            cols = (x - 1,)
            d = column(diag, cols, y - 1)
            txp, txl = column(txc, (x,), y - 1), column(txc, (x - 1,), y - 1)
            typ = column(tyc, cols, y)
            tzp, tzl = column(tzc, cols, y), column(tzm, cols, y - 1)
            if prev is None or prev[0] != y - 1:
                prev = (y - 1, column(tyc, cols, y - 1), [column(v, (k, x), y - 1) if halo or y > 1 else None for k in RHS],
                        [column(v, (k, x), y) for k in RHS])
            _, tyl, down, mid = prev
            up = [column(v, (k, x), y + 1) if halo or y < CY else None for k in RHS]
            for k in RHS:
                here = mid[k]
                out = d * here
                if halo or not (isinstance(x, int) and x == CX):
                    out = out - txp * column(v, (k, x + 1), y)
                if halo or not (isinstance(x, int) and x == 1):
                    out = out - txl * column(v, (k, x - 1), y)
                if up[k] is not None:
                    out = out - typ * up[k]
                if down[k] is not None:
                    out = out - tyl * down[k]
                out = out - (tzp * layer_above(v, (k, x), y, here, lane) + tzl * layer_below(v, (k, x), y, here, lane))
                put(k, x, y, out)
                if dots:
                    sums[k] = sums[k] + here * here
                    sums[K + k] = sums[K + k] + here * out
            prev = (y, typ, mid, up)
        return tuple(sums)

    def put_q(k, x, y, out):
        q[k, x, pl.ds(8 * y, 8), :] = out

    def put_end(k, x, y, out):
        put_q(k, x, y, out)
        if y in (1, CY):
            return
        send_x[0 if x == 1 else 1, k, pl.ds(8 * (y - 1), 8), :] = out

    def put_side(k, x, y, out):
        put_q(k, x, y, out)
        send_y[0 if y == 1 else 1, k, x - 1] = out

    def put_w(k, x, y, out):
        w[k, x - 1, pl.ds(8 * (y - 1), 8), :] = out

    def ends(v, put, sums, **kw):
        for x in (1, CX):
            sums = apply(v, put, x, range(1, CY + 1), sums, **kw)
        return sums

    def sides(v, put, sums, **kw):
        def at(i, s):
            for j in range(7):
                s = apply(v, put, 2 + 7 * i + j, (1, CY), s, **kw)
            return s
        return lax.fori_loop(0, 2, at, sums)

    none = tuple(jnp.zeros((8, 128), F32) for _ in range(2 * K))
    planes = pl.ds(8, 8 * CY)
    inside_y = pl.ds(16, 8 * (CY - 2))
    inside_x = pl.ds(2, CX - 2)
    all_x = pl.ds(1, CX)

    both = ((1, CX + 1, 0, 0, down_x), (CX, 0, 1, CX, up_x))
    both_y = ((low, after, 0, 1, down_y), (high, before, 1, CY, up_y))

    gather(pl.ds(0, 2 * K * CY))
    begin(0)
    begin(CX - 1)
    tips = []
    for i, (x, to_x, _, _, x_axis) in enumerate(both):
        for j, (y, to_y, _, _, y_axis) in enumerate(both_y):
            at = 10 + 4 * i + 2 * j
            tips.append(face(b.at[:, x, y], b.at[:, to_x, y], at, "gx", x_axis))
            tips.append(face(b.at[:, x, y], b.at[:, x, to_y], at + 1, "gy", y_axis))
    for c in tips:
        c.start()
    bx = [face(b.at[:, x, inside_y], b.at[:, to_x, inside_y], 2 + i, "gx", axis)
          for i, (x, to_x, _, _, axis) in enumerate(both)]
    for c in bx:
        c.start()
    by = []
    for part, some in enumerate((range(1, CX // 2), range(CX // 2, CX - 1))):
        gather(pl.ds(block(some[0]), len(some) * K * CY))
        loop(some[0], some[-1] + 1, begin)
        here = pl.ds(some[0] + 1, len(some))
        for i, (y, to_y, _, _, axis) in enumerate(both_y):
            c = face(b.at[:, here, y], b.at[:, here, to_y], (4 if part == 0 else 22) + i, "gy", axis)
            c.start()
            by.append(c)

    ends(b, put_end, none, halo=False, dots=False)
    sides(b, put_side, none, halo=False, dots=False)
    for c in tips:
        c.wait()
    for x, _, i, x_edge, _ in both:
        for _, _, j, y, _ in both_y:
            for k in RHS:
                here = column(q, (k, x), y)
                far_y = column(tyc, (x - 1,), 0 if y == 1 else CY) * column(b, (k, x), 0 if y == 1 else CY + 1)
                far_x = column(txc, (x_edge,), y - 1) * column(b, (k, 0 if x == 1 else CX + 1), y)
                send_x[i, k, pl.ds(8 * (y - 1), 8), :] = here - far_y
                send_y[j, k, x - 1] = here - far_x
    qy = [face(send_y.at[j], q.at[:, all_x, to_y], 8 + j, "gy", axis)
          for j, (_, to_y, _, _, axis) in enumerate(both_y)]
    for c in qy:
        c.start()
    first_half, second_half = [], []
    for i, (_, to_x, _, _, axis) in enumerate(both):
        for half in range(2):
            ks = pl.ds(2 * half, 2)
            c = face(send_x.at[i, ks], q.at[ks, to_x, planes], 18 + 2 * i + half, "gx", axis)
            (second_half if i == half else first_half).append(c)
    one = lax.fori_loop(2, 6, lambda x, s: apply(b, put_q, x, range(2, CY), s), none)
    for c in first_half:
        c.start()
    one = lax.fori_loop(6, CX, lambda x, s: apply(b, put_q, x, range(2, CY), s), one)

    two = lax.fori_loop(3, CX - 1, lambda x, s: apply(q, put_w, x, range(3, CY - 1), s), none)

    def complete(x, y, sums):
        sums = list(sums)
        for k in RHS:
            here = column(b, (k, x), y)
            out = column(q, (k, x), y)
            if isinstance(x, int):
                edge = 0 if x == 1 else CX
                out = out - column(txc, (edge,), y - 1) * column(b, (k, 0 if x == 1 else CX + 1), y)
            if y == 1:
                out = out - column(tyc, (x - 1,), 0) * column(b, (k, x), 0)
            if y == CY:
                out = out - column(tyc, (x - 1,), CY) * column(b, (k, x), CY + 1)
            put_q(k, x, y, out)
            sums[k] = sums[k] + here * here
            sums[K + k] = sums[K + k] + here * out
        return tuple(sums)

    for c in by + bx:
        c.wait()
    for x in (1, CX):
        for y in range(1, CY + 1):
            one = complete(x, y, one)
    one = lax.fori_loop(2, CX, lambda x, s: complete(x, CY, complete(x, 1, s)), one)
    for c in second_half:
        c.start()

    def ring(i, s):
        for j in range(4):
            s = apply(q, put_w, 3 + 4 * i + j, (1, 2, CY - 1, CY), s, halo=False)
        return s

    two = lax.fori_loop(0, (CX - 4) // 4, ring, two)
    for x in (1, 2, CX - 1, CX):
        two = apply(q, put_w, x, range(1, CY + 1), two, halo=False)

    def meet(k, x, y, t, far, sums):
        other = t * (far - t * column(b, (k, x), y))
        at = (k, x - 1, pl.ds(8 * (y - 1), 8), slice(None))
        w[at] = w[at] - other
        if sums is not None:
            sums[K + k] = sums[K + k] - 2.0 * (column(q, (k, x), y) * other)

    def meet_x(i, ks, sums):
        x, x_far, edge = ((1, 0, 0), (CX, CX + 1, CX))[i]
        for y in range(1, CY + 1):
            t = column(txc, (edge,), y - 1)
            for k in ks:
                meet(k, x, y, t, column(q, (k, x_far), y), sums)

    def meet_y(y, x, sums):
        t = column(tyc, (x - 1,), 0 if y == 1 else CY)
        for k in RHS:
            meet(k, x, y, t, column(q, (k, x), 0 if y == 1 else CY + 1), sums)

    for c in qy:
        c.wait()

    def lower_y(i, sums):
        sums = list(sums)
        for j in range(4):
            meet_y(1, 1 + 4 * i + j, sums)
        return tuple(sums)

    two = list(lax.fori_loop(0, CX // 4, lower_y, two))
    for c in first_half:
        c.wait()
    meet_x(0, (0, 1), two)
    meet_x(1, (2, 3), two)
    two = tuple(two)

    lane1 = lax.broadcasted_iota(jnp.int32, (1, 128), 1)
    line = jnp.zeros((1, 128), F32)
    for i, s in enumerate(one + two):
        line = jnp.where(lane1 == i, jnp.sum(s, keepdims=True), line)
    red_out[0] = line
    red1[gx] = line
    hops = []
    for d in range(1, NGX):
        to = lax.rem(gx + d, NGX)
        hops.append(remote(red_out.at[0], red1.at[gx], as1.at[d], ar1.at[d], "gx", to))
    for c in hops:
        c.start()
    loop(1, CX + 1, lambda x: meet_y(CY, x, None))
    for c in second_half:
        c.wait()
    meet_x(0, (2, 3), None)
    meet_x(1, (0, 1), None)
    for c in hops:
        c.wait()
    line = jnp.sum(red1[...], axis=0)
    red_out[1] = line
    red2[gy] = line
    hops = []
    for d in range(1, NGY):
        to = lax.rem(gy + d, NGY)
        hops.append(remote(red_out.at[1], red2.at[gy], as2.at[d], ar2.at[d], "gy", to))
    for c in hops:
        c.start()
    for c in hops:
        c.wait()
    line = jnp.sum(red2[...], axis=0)

    rr = line
    bq = pltpu.roll(line, 128 - K, 1)
    qq = pltpu.roll(line, 128 - 2 * K, 1)
    qw = pltpu.roll(line, 128 - 3 * K, 1)
    step0 = rr / bq
    rr1 = step0 * step0 * qq - rr
    grow = 1.0 + rr1 / rr
    step1 = rr1 / (grow * grow * bq - 2.0 * grow * step0 * qq + step0 * step0 * qw)
    sp[0] = step0 + step1 * grow
    sp[1] = step0 * step1


def last_kernel(b, q, w, sp, x_h, r_h, xo, ro, sem):
    ones = [jnp.broadcast_to(sp[0][:, k : k + 1], (8, 128)) for k in RHS]
    twos = [jnp.broadcast_to(sp[1][:, k : k + 1], (8, 128)) for k in RHS]
    copies = []
    step = 2

    def at(x, _):
        for k in RHS:
            for t in range(2):
                for c in range(8):
                    bv = b[k, x + 1, pl.ds(8 + 64 * t + c, 8, stride=8), :]
                    qv = q[k, x + 1, pl.ds(8 + 64 * t + c, 8, stride=8), :]
                    wv = w[k, x, pl.ds(64 * t + c, 8, stride=8), :]
                    to = (k, x, pl.ds(8 * t, 8), pl.ds(128 * c, 128))
                    xo[to] = ones[k] * bv - twos[k] * qv
                    ro[to] = bv - ones[k] * qv + twos[k] * wv
        return 0

    for i in range(CX // step):
        lax.fori_loop(i * step, (i + 1) * step, at, 0)
        part = pl.ds(i * step, step)
        for j, (s, h) in enumerate(((xo, x_h), (ro, r_h))):
            c = pltpu.make_async_copy(s.at[:, part], h.at[:, part], sem.at[2 * i + j])
            c.start()
            copies.append(c)
    for c in copies:
        c.wait()


def body(next_adjoint, accumulation, trans_x, trans_y, trans_z,
         well_owner, well_site, perf_layers, perf_count, well_index, misfit):
    dma = pltpu.SemaphoreType.DMA
    vm = pltpu.VMEM
    field = (K, CX + 2, 8 * (CY + 2), 128)
    plane = (CX, 8 * CY, 128)
    anywhere = pl.BlockSpec(memory_space=pl.ANY)
    inside = pl.BlockSpec(memory_space=pltpu.VMEM)
    b, q, w, sp = pl.pallas_call(
        main_kernel,
        out_shape=(
            pltpu.VMEM(field, F32), pltpu.VMEM(field, F32), pltpu.VMEM((K, *plane), F32), pltpu.VMEM((2, 1, 128), F32),
        ),
        in_specs=[anywhere] * 11,
        out_specs=(inside,) * 4,
        scratch_shapes=[
            vm((K, CX, CY, NZ), F32), vm((4, CX, CY, NZ), F32), vm((K * CX * CY, NZ), F32),
            vm(plane, F32), vm((CX + 1, 8 * CY, 128), F32), vm((CX, 8 * CY + 8, 128), F32),
            vm((CX, 8 * CY + 8, 128), F32), vm(plane, F32),
            vm((1, WELLS), jnp.int32), vm((1, WELLS), jnp.int32), vm((PERF, WELLS), jnp.int32),
            vm((1, WELLS), jnp.int32), vm((PERF, WELLS), F32), vm((K, WELLS), F32),
            vm((128, WELLS), F32), vm((NGY, NGX, 128), F32), vm((NGY * NGX, 128), F32),
            vm((NGX, NGY, 128), F32), vm((NGX * NGY, 128), F32),
            vm((K * CX * CY, 384), BF16), vm((384, NZ), BF16),
            vm((2, K, 8 * CY, 128), F32), vm((2, K, CX, 8, 128), F32),
            vm((2, 1, 128), F32), vm((NGX, 1, 128), F32), vm((NGY, 1, 128), F32),
            dma((8,)), dma((6,)), dma((NGY,)), dma((NGY,)), dma((NGX,)), dma((NGX,)),
            dma((24,)), dma((24,)), dma((NGX,)), dma((NGX,)), dma((NGY,)), dma((NGY,)),
        ],
        compiler_params=pltpu.CompilerParams(
            collective_id=0, has_side_effects=True, vmem_limit_bytes=40 * 2**20),
        cost_estimate=pl.CostEstimate(flops=60_000_000, bytes_accessed=9_000_000, transcendentals=0),
        name="adjoint_krylov",
    )(next_adjoint, accumulation, trans_x, trans_y, trans_z, well_owner.T, well_site.reshape(1, WELLS),
      perf_layers.T, perf_count.reshape(1, WELLS), well_index.T, misfit.T)
    out = jax.ShapeDtypeStruct((K, CX, CY, NZ), F32)
    return pl.pallas_call(
        last_kernel,
        out_shape=(out, out),
        in_specs=[inside] * 4,
        out_specs=(anywhere, anywhere),
        scratch_shapes=[vm((K, CX, CY, NZ), F32), vm((K, CX, CY, NZ), F32), dma((16,))],
        compiler_params=pltpu.CompilerParams(vmem_limit_bytes=24 * 2**20),
        name="adjoint_result",
    )(b, q, w, sp)


def solution(mesh):
    flat = P(("gx", "gy"))
    rows_of = P(("gx", "gy"), None)
    cells = P("gx", "gy", None)
    many = P(None, "gx", "gy", None)
    return jax.shard_map(
        body,
        mesh=mesh,
        in_specs=(many, cells, cells, cells, cells, rows_of, flat, rows_of, flat, rows_of, rows_of),
        out_specs=(many, many),
        check_vma=False,
    )
```

```python
import jax
import jax.numpy as jnp
from jax import lax
from jax.experimental import pallas as pl
from jax.experimental.pallas import tpu as pltpu
from jax.sharding import PartitionSpec as P

F32 = jnp.float32
BF16 = jnp.bfloat16
MESH = pl.DeviceIdType.MESH
K, CX, CY, NZ = 4, 16, 16, 1024
NGX, NGY = 16, 8
PERF, WELLS = 16, 64
RHS = range(K)


def remote(src, dst, send, recv, axis, index):
    return pltpu.make_async_remote_copy(
        src_ref=src, dst_ref=dst, send_sem=send, recv_sem=recv,
        device_id={axis: index}, device_id_type=MESH,
    )


def lanes():
    return lax.broadcasted_iota(jnp.int32, (8, 128), 1)


def rows():
    return lax.broadcasted_iota(jnp.int32, (8, 128), 0)


def column(ref, lead, y):
    return ref[(*lead, pl.ds(8 * y, 8), slice(None))]


def layer_above(ref, lead, y, here, lane):
    nxt = pltpu.roll(here, 7, 0) if y == CY else ref[(*lead, pl.ds(8 * y + 1, 8), slice(None))]
    return pltpu.roll(jnp.where(lane == 0, nxt, here), 127, 1)


def layer_below(ref, lead, y, here, lane):
    prv = pltpu.roll(here, 1, 0) if y == 1 else ref[(*lead, pl.ds(8 * y - 1, 8), slice(None))]
    return pltpu.roll(jnp.where(lane == 127, prv, here), 1, 1)


def main_kernel(
    na_h, acc_h, tx_h, ty_h, tz_h, own_h, site_h, lay_h, cnt_h, wi_h, mis_h,
    b, q, w, sp,
    na, co, src, diag, txc, tyc, tzc, tzm,
    own, site, lay, cnt, wi, mis, packed, out1, in1, out2, in2, left, right, send_x, send_y, red_out, red1, red2,
    load_sem, well_sem, s1, r1, s2, r2, hs, hr, as1, ar1, as2, ar2,
):
    gx, gy = lax.axis_index("gx"), lax.axis_index("gy")
    up_x, down_x = lax.rem(gx + 1, NGX), lax.rem(gx + NGX - 1, NGX)
    up_y, down_y = lax.rem(gy + 1, NGY), lax.rem(gy + NGY - 1, NGY)

    wells = [pltpu.make_async_copy(h, v, well_sem.at[i]) for i, (h, v) in enumerate(
        ((own_h, own), (site_h, site), (lay_h, lay), (cnt_h, cnt), (wi_h, wi), (mis_h, mis)))]
    for c in wells:
        c.start()
    barrier = pltpu.get_barrier_semaphore()
    for d in range(1, NGY):
        pl.semaphore_signal(barrier, inc=1, device_id={"gy": lax.rem(gy + d, NGY)}, device_id_type=MESH)
    for d in range(1, NGX):
        pl.semaphore_signal(barrier, inc=1, device_id={"gx": lax.rem(gx + d, NGX)}, device_id_type=MESH)

    for c in wells:
        c.wait()
    used = lax.broadcasted_iota(jnp.int32, (PERF, WELLS), 0) < cnt[...]
    packed[...] = jnp.zeros_like(packed)
    packed[0:16, :] = jnp.where(used, wi[...], 0.0)
    packed[16:32, :] = lay[...].astype(F32)
    packed[32:36, :] = mis[...]
    packed[36:37, :] = site[...].astype(F32)
    owner = own[...]
    place = lax.rem(owner, NGY) * NGX + owner // NGY
    onehot = jnp.where(lax.broadcasted_iota(jnp.int32, (128, WELLS), 0) == place, 1.0, 0.0).astype(F32)
    out1[...] = lax.dot_general(
        onehot, packed[...], (((1,), (1,)), ((), ())),
        precision=lax.Precision.HIGHEST, preferred_element_type=F32,
    ).reshape(NGY, NGX, 128)

    pl.semaphore_wait(barrier, NGX + NGY - 2)

    first = []
    for d in range(1, NGY):
        to = lax.rem(gy + d, NGY)
        first.append(remote(out1.at[to], in1.at[pl.ds(gy * NGX, NGX)], s1.at[d], r1.at[d], "gy", to))
    for c in first:
        c.start()
    coef = [pltpu.make_async_copy(h, co.at[i], load_sem.at[i]) for i, h in enumerate((tx_h, ty_h, tz_h, acc_h))]
    for c in coef:
        c.start()
    fields = [pltpu.make_async_copy(na_h.at[k], na.at[k], load_sem.at[4 + k]) for k in RHS]
    for c in fields:
        c.start()

    in1[pl.ds(gy * NGX, NGX), :] = out1[gy]

    last_x = gx == NGX - 1
    last_y = gy == NGY - 1

    def spread(i, put):
        def at(x, _):
            for t in range(2):
                for c in range(8):
                    put(x, t, c, co[i, x, pl.ds(8 * t, 8), pl.ds(128 * c, 128)])
            return 0
        coef[i].wait()
        lax.fori_loop(0, CX, at, 0)

    def put_x(x, t, c, v):
        txc[x + 1, pl.ds(64 * t + c, 8, stride=8), :] = jnp.where(last_x & (x == CX - 1), 0.0, v)

    def put_y(x, t, c, v):
        if t == 1:
            v = jnp.where(last_y & (rows() == 7), 0.0, v)
        tyc[x, pl.ds(8 + 64 * t + c, 8, stride=8), :] = v

    def put_z(x, t, c, v):
        if c == 7:
            v = jnp.where(lanes() == 127, 0.0, v)
        tzc[x, pl.ds(8 + 64 * t + c, 8, stride=8), :] = v

    def put_a(x, t, c, v):
        diag[x, pl.ds(64 * t + c, 8, stride=8), :] = v

    spread(0, put_x)
    face_tx = remote(txc.at[CX], txc.at[0], hs.at[0], hr.at[0], "gx", up_x)
    face_tx.start()
    spread(1, put_y)
    face_ty = remote(tyc.at[:, pl.ds(8 * CY, 8)], tyc.at[:, pl.ds(0, 8)], hs.at[1], hr.at[1], "gy", up_y)
    face_ty.start()

    for c in first:
        c.wait()
    for to in range(NGX):
        out2[to] = in1[pl.ds(to, NGY, stride=NGX), :]
    second = []
    for d in range(1, NGX):
        to = lax.rem(gx + d, NGX)
        second.append(remote(out2.at[to], in2.at[pl.ds(gx * NGY, NGY)], s2.at[d], r2.at[d], "gx", to))
    for c in second:
        c.start()
    in2[pl.ds(gx * NGY, NGY), :] = out2[gx]

    spread(2, put_z)
    spread(3, put_a)
    face_tx.wait()
    face_ty.wait()
    tzc[:, 0:8, :] = jnp.zeros((CX, 8, 128), F32)

    def diagonal(x, _):
        lane = lanes()
        start = (rows() == 0) & (lane == 0)
        ty_low = column(tyc, (x,), 0)
        for y in range(CY):
            here = column(tzc, (x,), y + 1)
            below = jnp.where(start, 0.0, layer_below(tzc, (x,), y + 1, here, lane))
            tzm[x, pl.ds(8 * y, 8), :] = below
            ty_here = column(tyc, (x,), y + 1)
            diag[x, pl.ds(8 * y, 8), :] = (
                column(diag, (x,), y) + (column(txc, (x + 1,), y) + column(txc, (x,), y))
                + (ty_here + ty_low) + (here + below)
            )
            ty_low = ty_here
        return 0

    lax.fori_loop(0, CX, diagonal, 0)

    def split(v):
        high = v.astype(BF16).astype(F32)
        return high, (v - high)

    def terms(t, _):
        lane = lanes().astype(F32)
        at = pl.ds(pl.multiple_of(16 * t, 16), 16)
        high, low = [], []
        for half in range(2):
            tile = in2[pl.ds(pl.multiple_of(16 * t + 8 * half, 8), 8), :]
            total = [jnp.zeros((8, 128), F32) for _ in range(8)]
            for p in range(PERF):
                value = jnp.broadcast_to(tile[:, p : p + 1], (8, 128))
                layer = jnp.broadcast_to(tile[:, 16 + p : 17 + p], (8, 128))
                for c in range(8):
                    total[c] = total[c] + jnp.where(layer == lane + 128.0 * c, value, 0.0)
            total = jnp.concatenate(total, axis=1)
            h, l = split(total)
            high.append(h)
            low.append(l)
        high = jnp.concatenate(high, axis=0).astype(BF16)
        right[at, :] = high
        right[pl.ds(pl.multiple_of(128 + 16 * t, 16), 16), :] = jnp.concatenate(low, axis=0).astype(BF16)
        right[pl.ds(pl.multiple_of(256 + 16 * t, 16), 16), :] = high
        return 0

    def arrived(source):
        d = lax.rem(gx + NGX - source, NGX)
        remote(out2.at[0], in2.at[pl.ds(source * NGY, NGY)], s2.at[d], r2.at[d], "gx", source).wait_recv()

    arrived(gx + 1 - 2 * lax.rem(gx, 2))
    terms(gx // 2, 0)

    def next_tile(j, _):
        i = j // 2
        t = 2 * lax.rem(gx // 4 + i * (i + 1) // 2, 4) + lax.rem(lax.rem(gx, 4) // 2 + j, 2)
        arrived(2 * t)
        arrived(2 * t + 1)
        return terms(t, 0)

    lax.fori_loop(1, NGX // 2, next_tile, 0)
    for c in second:
        c.wait_send()


    def block(x):
        if isinstance(x, int):
            return K * CY * (0 if x == 0 else 1 if x == CX - 1 else x + 1)
        return pl.multiple_of(K * CY * (x + 1), K * CY)

    across = in2[...].T

    mis_high, mis_low = split(across[32:36, :])
    for x in range(CX):
        spot = (lax.broadcasted_iota(jnp.int32, (CY, 128), 0) + CY * x).astype(F32) == across[36:37, :]
        for k in RHS:
            at = pl.ds(block(x) + CY * k, CY)
            high = jnp.where(spot, mis_high[k : k + 1, :], 0.0).astype(BF16)
            left[at, 0:128] = high
            left[at, 128:256] = high
            left[at, 256:384] = jnp.where(spot, mis_low[k : k + 1, :], 0.0).astype(BF16)

    def gather(part):
        def at(n, _):
            here = pl.ds(pl.multiple_of(256 * n, 256), 256)
            src[part, here] = jnp.dot(left[part, :], right[:, here], preferred_element_type=F32)
            return 0
        lax.fori_loop(0, NZ // 256, at, 0)

    for c in fields:
        c.wait()

    def begin(x):
        for k in RHS:
            for t in range(2):
                for c in range(8):
                    at = (pl.ds(8 * t, 8), pl.ds(128 * c, 128))
                    row = block(x) + (CY * k + 8 * t)
                    row = row if isinstance(x, int) else pl.multiple_of(row, 8)
                    v = co[3, x, *at] * na[k, x, *at] + src[pl.ds(row, 8), pl.ds(128 * c, 128)]
                    b[k, x + 1, pl.ds(8 + 64 * t + c, 8, stride=8), :] = v

    def face(src_ref, dst_ref, at, axis, to):
        return remote(src_ref, dst_ref, hs.at[at], hr.at[at], axis, to)

    low, high = pl.ds(8, 8), pl.ds(8 * CY, 8)
    before, after = pl.ds(0, 8), pl.ds(8 * CY + 8, 8)

    def loop(lo, hi, fn):
        def body(x, _):
            fn(x)
            return 0
        lax.fori_loop(lo, hi, body, 0)

    def apply(v, put, x, ys, sums, halo=True, dots=True):
        lane = lanes()
        sums = list(sums)
        prev = None
        for y in ys:
            cols = (x - 1,)
            d = column(diag, cols, y - 1)
            txp, txl = column(txc, (x,), y - 1), column(txc, (x - 1,), y - 1)
            typ = column(tyc, cols, y)
            tzp, tzl = column(tzc, cols, y), column(tzm, cols, y - 1)
            if prev is None or prev[0] != y - 1:
                prev = (y - 1, column(tyc, cols, y - 1), [column(v, (k, x), y - 1) if halo or y > 1 else None for k in RHS],
                        [column(v, (k, x), y) for k in RHS])
            _, tyl, down, mid = prev
            up = [column(v, (k, x), y + 1) if halo or y < CY else None for k in RHS]
            for k in RHS:
                here = mid[k]
                out = d * here
                if halo or not (isinstance(x, int) and x == CX):
                    out = out - txp * column(v, (k, x + 1), y)
                if halo or not (isinstance(x, int) and x == 1):
                    out = out - txl * column(v, (k, x - 1), y)
                if up[k] is not None:
                    out = out - typ * up[k]
                if down[k] is not None:
                    out = out - tyl * down[k]
                out = out - (tzp * layer_above(v, (k, x), y, here, lane) + tzl * layer_below(v, (k, x), y, here, lane))
                put(k, x, y, out)
                if dots:
                    sums[k] = sums[k] + here * here
                    sums[K + k] = sums[K + k] + here * out
            prev = (y, typ, mid, up)
        return tuple(sums)

    def put_q(k, x, y, out):
        q[k, x, pl.ds(8 * y, 8), :] = out

    def put_end(k, x, y, out):
        put_q(k, x, y, out)
        if y in (1, CY):
            return
        send_x[0 if x == 1 else 1, k, pl.ds(8 * (y - 1), 8), :] = out

    def put_side(k, x, y, out):
        put_q(k, x, y, out)
        send_y[0 if y == 1 else 1, k, x - 1] = out

    def put_w(k, x, y, out):
        w[k, x - 1, pl.ds(8 * (y - 1), 8), :] = out

    def ends(v, put, sums, **kw):
        for x in (1, CX):
            sums = apply(v, put, x, range(1, CY + 1), sums, **kw)
        return sums

    def sides(v, put, sums, **kw):
        def at(i, s):
            for j in range(7):
                s = apply(v, put, 2 + 7 * i + j, (1, CY), s, **kw)
            return s
        return lax.fori_loop(0, 2, at, sums)

    none = tuple(jnp.zeros((8, 128), F32) for _ in range(2 * K))
    planes = pl.ds(8, 8 * CY)
    inside_y = pl.ds(16, 8 * (CY - 2))
    inside_x = pl.ds(2, CX - 2)
    all_x = pl.ds(1, CX)

    both = ((1, CX + 1, 0, 0, down_x), (CX, 0, 1, CX, up_x))
    both_y = ((low, after, 0, 1, down_y), (high, before, 1, CY, up_y))

    gather(pl.ds(0, 2 * K * CY))
    begin(0)
    begin(CX - 1)
    tips = []
    for i, (x, to_x, _, _, x_axis) in enumerate(both):
        for j, (y, to_y, _, _, y_axis) in enumerate(both_y):
            at = 10 + 4 * i + 2 * j
            tips.append(face(b.at[:, x, y], b.at[:, to_x, y], at, "gx", x_axis))
            tips.append(face(b.at[:, x, y], b.at[:, x, to_y], at + 1, "gy", y_axis))
    for c in tips:
        c.start()
    bx = [face(b.at[:, x, inside_y], b.at[:, to_x, inside_y], 2 + i, "gx", axis)
          for i, (x, to_x, _, _, axis) in enumerate(both)]
    for c in bx:
        c.start()
    by = []
    for part, some in enumerate((range(1, CX // 2), range(CX // 2, CX - 1))):
        gather(pl.ds(block(some[0]), len(some) * K * CY))
        loop(some[0], some[-1] + 1, begin)
        here = pl.ds(some[0] + 1, len(some))
        for i, (y, to_y, _, _, axis) in enumerate(both_y):
            c = face(b.at[:, here, y], b.at[:, here, to_y], (4 if part == 0 else 22) + i, "gy", axis)
            c.start()
            by.append(c)

    ends(b, put_end, none, halo=False, dots=False)
    sides(b, put_side, none, halo=False, dots=False)
    for c in tips:
        c.wait()
    for x, _, i, x_edge, _ in both:
        for _, _, j, y, _ in both_y:
            for k in RHS:
                here = column(q, (k, x), y)
                far_y = column(tyc, (x - 1,), 0 if y == 1 else CY) * column(b, (k, x), 0 if y == 1 else CY + 1)
                far_x = column(txc, (x_edge,), y - 1) * column(b, (k, 0 if x == 1 else CX + 1), y)
                send_x[i, k, pl.ds(8 * (y - 1), 8), :] = here - far_y
                send_y[j, k, x - 1] = here - far_x
    qy = [face(send_y.at[j], q.at[:, all_x, to_y], 8 + j, "gy", axis)
          for j, (_, to_y, _, _, axis) in enumerate(both_y)]
    for c in qy:
        c.start()
    first_half, second_half = [], []
    for i, (_, to_x, _, _, axis) in enumerate(both):
        for half in range(2):
            ks = pl.ds(2 * half, 2)
            c = face(send_x.at[i, ks], q.at[ks, to_x, planes], 18 + 2 * i + half, "gx", axis)
            (second_half if i == half else first_half).append(c)
    one = lax.fori_loop(2, 6, lambda x, s: apply(b, put_q, x, range(2, CY), s), none)
    for c in first_half:
        c.start()
    one = lax.fori_loop(6, CX, lambda x, s: apply(b, put_q, x, range(2, CY), s), one)

    two = lax.fori_loop(3, CX - 1, lambda x, s: apply(q, put_w, x, range(3, CY - 1), s), none)

    def complete(x, y, sums):
        sums = list(sums)
        for k in RHS:
            here = column(b, (k, x), y)
            out = column(q, (k, x), y)
            if isinstance(x, int):
                edge = 0 if x == 1 else CX
                out = out - column(txc, (edge,), y - 1) * column(b, (k, 0 if x == 1 else CX + 1), y)
            if y == 1:
                out = out - column(tyc, (x - 1,), 0) * column(b, (k, x), 0)
            if y == CY:
                out = out - column(tyc, (x - 1,), CY) * column(b, (k, x), CY + 1)
            put_q(k, x, y, out)
            sums[k] = sums[k] + here * here
            sums[K + k] = sums[K + k] + here * out
        return tuple(sums)

    for c in by + bx:
        c.wait()
    for x in (1, CX):
        for y in range(1, CY + 1):
            one = complete(x, y, one)
    one = lax.fori_loop(2, CX, lambda x, s: complete(x, CY, complete(x, 1, s)), one)
    for c in second_half:
        c.start()

    def ring(i, s):
        for j in range(4):
            s = apply(q, put_w, 3 + 4 * i + j, (1, 2, CY - 1, CY), s, halo=False)
        return s

    two = lax.fori_loop(0, (CX - 4) // 4, ring, two)
    for x in (1, 2, CX - 1, CX):
        two = apply(q, put_w, x, range(1, CY + 1), two, halo=False)

    def meet(k, x, y, t, far, sums):
        other = t * (far - t * column(b, (k, x), y))
        at = (k, x - 1, pl.ds(8 * (y - 1), 8), slice(None))
        w[at] = w[at] - other
        if sums is not None:
            sums[K + k] = sums[K + k] - 2.0 * (column(q, (k, x), y) * other)

    def meet_x(i, ks, sums):
        x, x_far, edge = ((1, 0, 0), (CX, CX + 1, CX))[i]
        for y in range(1, CY + 1):
            t = column(txc, (edge,), y - 1)
            for k in ks:
                meet(k, x, y, t, column(q, (k, x_far), y), sums)

    def meet_y(y, x, sums):
        t = column(tyc, (x - 1,), 0 if y == 1 else CY)
        for k in RHS:
            meet(k, x, y, t, column(q, (k, x), 0 if y == 1 else CY + 1), sums)

    for c in qy:
        c.wait()

    def lower_y(i, sums):
        sums = list(sums)
        for j in range(4):
            meet_y(1, 1 + 4 * i + j, sums)
        return tuple(sums)

    two = list(lax.fori_loop(0, CX // 4, lower_y, two))
    for c in first_half:
        c.wait()
    meet_x(0, (0, 1), two)
    meet_x(1, (2, 3), two)
    two = tuple(two)

    lane1 = lax.broadcasted_iota(jnp.int32, (1, 128), 1)
    line = jnp.zeros((1, 128), F32)
    for i, s in enumerate(one + two):
        line = jnp.where(lane1 == i, jnp.sum(s, keepdims=True), line)
    red_out[0] = line
    red1[gx] = line
    hops = []
    for d in range(1, NGX):
        to = lax.rem(gx + d, NGX)
        hops.append(remote(red_out.at[0], red1.at[gx], as1.at[d], ar1.at[d], "gx", to))
    for c in hops:
        c.start()
    loop(1, CX + 1, lambda x: meet_y(CY, x, None))
    for c in second_half:
        c.wait()
    meet_x(0, (2, 3), None)
    meet_x(1, (0, 1), None)
    for c in hops:
        c.wait()
    line = jnp.sum(red1[...], axis=0)
    red_out[1] = line
    red2[gy] = line
    hops = []
    for d in range(1, NGY):
        to = lax.rem(gy + d, NGY)
        hops.append(remote(red_out.at[1], red2.at[gy], as2.at[d], ar2.at[d], "gy", to))
    for c in hops:
        c.start()
    for c in hops:
        c.wait()
    line = jnp.sum(red2[...], axis=0)

    rr = line
    bq = pltpu.roll(line, 128 - K, 1)
    qq = pltpu.roll(line, 128 - 2 * K, 1)
    qw = pltpu.roll(line, 128 - 3 * K, 1)
    step0 = rr / bq
    rr1 = step0 * step0 * qq - rr
    grow = 1.0 + rr1 / rr
    step1 = rr1 / (grow * grow * bq - 2.0 * grow * step0 * qq + step0 * step0 * qw)
    sp[0] = step0 + step1 * grow
    sp[1] = step0 * step1


def last_kernel(b, q, w, sp, x_h, r_h, xo, ro, sem):
    ones = [jnp.broadcast_to(sp[0][:, k : k + 1], (8, 128)) for k in RHS]
    twos = [jnp.broadcast_to(sp[1][:, k : k + 1], (8, 128)) for k in RHS]
    copies = []
    step = 2

    def at(x, _):
        for k in RHS:
            for t in range(2):
                for c in range(8):
                    bv = b[k, x + 1, pl.ds(8 + 64 * t + c, 8, stride=8), :]
                    qv = q[k, x + 1, pl.ds(8 + 64 * t + c, 8, stride=8), :]
                    wv = w[k, x, pl.ds(64 * t + c, 8, stride=8), :]
                    to = (k, x, pl.ds(8 * t, 8), pl.ds(128 * c, 128))
                    xo[to] = ones[k] * bv - twos[k] * qv
                    ro[to] = bv - ones[k] * qv + twos[k] * wv
        return 0

    for i in range(CX // step):
        lax.fori_loop(i * step, (i + 1) * step, at, 0)
        part = pl.ds(i * step, step)
        for j, (s, h) in enumerate(((xo, x_h), (ro, r_h))):
            c = pltpu.make_async_copy(s.at[:, part], h.at[:, part], sem.at[2 * i + j])
            c.start()
            copies.append(c)
    for c in copies:
        c.wait()


def body(next_adjoint, accumulation, trans_x, trans_y, trans_z,
         well_owner, well_site, perf_layers, perf_count, well_index, misfit):
    dma = pltpu.SemaphoreType.DMA
    vm = pltpu.VMEM
    field = (K, CX + 2, 8 * (CY + 2), 128)
    plane = (CX, 8 * CY, 128)
    anywhere = pl.BlockSpec(memory_space=pl.ANY)
    inside = pl.BlockSpec(memory_space=pltpu.VMEM)
    b, q, w, sp = pl.pallas_call(
        main_kernel,
        out_shape=(
            pltpu.VMEM(field, F32), pltpu.VMEM(field, F32), pltpu.VMEM((K, *plane), F32), pltpu.VMEM((2, 1, 128), F32),
        ),
        in_specs=[anywhere] * 11,
        out_specs=(inside,) * 4,
        scratch_shapes=[
            vm((K, CX, CY, NZ), F32), vm((4, CX, CY, NZ), F32), vm((K * CX * CY, NZ), F32),
            vm(plane, F32), vm((CX + 1, 8 * CY, 128), F32), vm((CX, 8 * CY + 8, 128), F32),
            vm((CX, 8 * CY + 8, 128), F32), vm(plane, F32),
            vm((1, WELLS), jnp.int32), vm((1, WELLS), jnp.int32), vm((PERF, WELLS), jnp.int32),
            vm((1, WELLS), jnp.int32), vm((PERF, WELLS), F32), vm((K, WELLS), F32),
            vm((128, WELLS), F32), vm((NGY, NGX, 128), F32), vm((NGY * NGX, 128), F32),
            vm((NGX, NGY, 128), F32), vm((NGX * NGY, 128), F32),
            vm((K * CX * CY, 384), BF16), vm((384, NZ), BF16),
            vm((2, K, 8 * CY, 128), F32), vm((2, K, CX, 8, 128), F32),
            vm((2, 1, 128), F32), vm((NGX, 1, 128), F32), vm((NGY, 1, 128), F32),
            dma((8,)), dma((6,)), dma((NGY,)), dma((NGY,)), dma((NGX,)), dma((NGX,)),
            dma((24,)), dma((24,)), dma((NGX,)), dma((NGX,)), dma((NGY,)), dma((NGY,)),
        ],
        compiler_params=pltpu.CompilerParams(
            collective_id=0, has_side_effects=True, vmem_limit_bytes=40 * 2**20),
        cost_estimate=pl.CostEstimate(flops=60_000_000, bytes_accessed=9_000_000, transcendentals=0),
        name="adjoint_krylov",
    )(next_adjoint, accumulation, trans_x, trans_y, trans_z, well_owner.T, well_site.reshape(1, WELLS),
      perf_layers.T, perf_count.reshape(1, WELLS), well_index.T, misfit.T)
    out = jax.ShapeDtypeStruct((K, CX, CY, NZ), F32)
    return pl.pallas_call(
        last_kernel,
        out_shape=(out, out),
        in_specs=[inside] * 4,
        out_specs=(anywhere, anywhere),
        scratch_shapes=[vm((K, CX, CY, NZ), F32), vm((K, CX, CY, NZ), F32), dma((16,))],
        compiler_params=pltpu.CompilerParams(vmem_limit_bytes=24 * 2**20),
        name="adjoint_result",
    )(b, q, w, sp)


def solution(mesh):
    flat = P(("gx", "gy"))
    rows_of = P(("gx", "gy"), None)
    cells = P("gx", "gy", None)
    many = P(None, "gx", "gy", None)
    return jax.shard_map(
        body,
        mesh=mesh,
        in_specs=(many, cells, cells, cells, cells, rows_of, flat, rows_of, flat, rows_of, rows_of),
        out_specs=(many, many),
        check_vma=False,
    )
```

```python
import jax
import jax.numpy as jnp
from jax import lax
from jax.experimental import pallas as pl
from jax.experimental.pallas import tpu as pltpu
from jax.sharding import PartitionSpec as P

F32 = jnp.float32
BF16 = jnp.bfloat16
MESH = pl.DeviceIdType.MESH
K, CX, CY, NZ = 4, 16, 16, 1024
NGX, NGY = 16, 8
PERF, WELLS = 16, 64
RHS = range(K)


def remote(src, dst, send, recv, axis, index):
    return pltpu.make_async_remote_copy(
        src_ref=src, dst_ref=dst, send_sem=send, recv_sem=recv,
        device_id={axis: index}, device_id_type=MESH,
    )


def lanes():
    return lax.broadcasted_iota(jnp.int32, (8, 128), 1)


def rows():
    return lax.broadcasted_iota(jnp.int32, (8, 128), 0)


def column(ref, lead, y):
    return ref[(*lead, pl.ds(8 * y, 8), slice(None))]


def layer_above(ref, lead, y, here, lane):
    nxt = pltpu.roll(here, 7, 0) if y == CY else ref[(*lead, pl.ds(8 * y + 1, 8), slice(None))]
    return pltpu.roll(jnp.where(lane == 0, nxt, here), 127, 1)


def layer_below(ref, lead, y, here, lane):
    prv = pltpu.roll(here, 1, 0) if y == 1 else ref[(*lead, pl.ds(8 * y - 1, 8), slice(None))]
    return pltpu.roll(jnp.where(lane == 127, prv, here), 1, 1)


def main_kernel(
    na_h, acc_h, tx_h, ty_h, tz_h, own_h, site_h, lay_h, cnt_h, wi_h, mis_h,
    b, q, w, sp,
    na, co, src, diag, txc, tyc, tzc, tzm,
    own, site, lay, cnt, wi, mis, packed, out1, in1, out2, in2, left, right, send_x, send_y, red_out, red1, red2,
    load_sem, well_sem, s1, r1, s2, r2, hs, hr, as1, ar1, as2, ar2,
):
    gx, gy = lax.axis_index("gx"), lax.axis_index("gy")
    up_x, down_x = lax.rem(gx + 1, NGX), lax.rem(gx + NGX - 1, NGX)
    up_y, down_y = lax.rem(gy + 1, NGY), lax.rem(gy + NGY - 1, NGY)

    wells = [pltpu.make_async_copy(h, v, well_sem.at[i]) for i, (h, v) in enumerate(
        ((own_h, own), (site_h, site), (lay_h, lay), (cnt_h, cnt), (wi_h, wi), (mis_h, mis)))]
    for c in wells:
        c.start()
    barrier = pltpu.get_barrier_semaphore()
    for d in range(1, NGY):
        pl.semaphore_signal(barrier, inc=1, device_id={"gy": lax.rem(gy + d, NGY)}, device_id_type=MESH)
    for d in range(1, NGX):
        pl.semaphore_signal(barrier, inc=1, device_id={"gx": lax.rem(gx + d, NGX)}, device_id_type=MESH)

    for c in wells:
        c.wait()
    used = lax.broadcasted_iota(jnp.int32, (PERF, WELLS), 0) < cnt[...]
    packed[...] = jnp.zeros_like(packed)
    packed[0:16, :] = jnp.where(used, wi[...], 0.0)
    packed[16:32, :] = lay[...].astype(F32)
    packed[32:36, :] = mis[...]
    packed[36:37, :] = site[...].astype(F32)
    owner = own[...]
    place = lax.rem(owner, NGY) * NGX + owner // NGY
    onehot = jnp.where(lax.broadcasted_iota(jnp.int32, (128, WELLS), 0) == place, 1.0, 0.0).astype(F32)
    out1[...] = lax.dot_general(
        onehot, packed[...], (((1,), (1,)), ((), ())),
        precision=lax.Precision.HIGHEST, preferred_element_type=F32,
    ).reshape(NGY, NGX, 128)

    pl.semaphore_wait(barrier, NGX + NGY - 2)

    first = []
    for d in range(1, NGY):
        to = lax.rem(gy + d, NGY)
        first.append(remote(out1.at[to], in1.at[pl.ds(gy * NGX, NGX)], s1.at[d], r1.at[d], "gy", to))
    for c in first:
        c.start()
    coef = [pltpu.make_async_copy(h, co.at[i], load_sem.at[i]) for i, h in enumerate((tx_h, ty_h, tz_h, acc_h))]
    for c in coef:
        c.start()
    fields = [pltpu.make_async_copy(na_h.at[k], na.at[k], load_sem.at[4 + k]) for k in RHS]

    in1[pl.ds(gy * NGX, NGX), :] = out1[gy]

    last_x = gx == NGX - 1
    last_y = gy == NGY - 1

    def spread(i, put):
        def at(x, _):
            for t in range(2):
                for c in range(8):
                    put(x, t, c, co[i, x, pl.ds(8 * t, 8), pl.ds(128 * c, 128)])
            return 0
        coef[i].wait()
        lax.fori_loop(0, CX, at, 0)

    def put_x(x, t, c, v):
        txc[x + 1, pl.ds(64 * t + c, 8, stride=8), :] = jnp.where(last_x & (x == CX - 1), 0.0, v)

    def put_y(x, t, c, v):
        if t == 1:
            v = jnp.where(last_y & (rows() == 7), 0.0, v)
        tyc[x, pl.ds(8 + 64 * t + c, 8, stride=8), :] = v

    def put_z(x, t, c, v):
        if c == 7:
            v = jnp.where(lanes() == 127, 0.0, v)
        tzc[x, pl.ds(8 + 64 * t + c, 8, stride=8), :] = v

    def put_a(x, t, c, v):
        diag[x, pl.ds(64 * t + c, 8, stride=8), :] = v

    spread(0, put_x)
    face_tx = remote(txc.at[CX], txc.at[0], hs.at[0], hr.at[0], "gx", up_x)
    face_tx.start()
    spread(1, put_y)
    face_ty = remote(tyc.at[:, pl.ds(8 * CY, 8)], tyc.at[:, pl.ds(0, 8)], hs.at[1], hr.at[1], "gy", up_y)
    face_ty.start()

    for c in first:
        c.wait()
    for to in range(NGX):
        out2[to] = in1[pl.ds(to, NGY, stride=NGX), :]
    second = []
    for d in range(1, NGX):
        to = lax.rem(gx + d, NGX)
        second.append(remote(out2.at[to], in2.at[pl.ds(gx * NGY, NGY)], s2.at[d], r2.at[d], "gx", to))
    for c in second:
        c.start()
    for c in fields:
        c.start()
    in2[pl.ds(gx * NGY, NGY), :] = out2[gx]

    spread(2, put_z)
    spread(3, put_a)
    face_tx.wait()
    face_ty.wait()
    tzc[:, 0:8, :] = jnp.zeros((CX, 8, 128), F32)

    def diagonal(x, _):
        lane = lanes()
        start = (rows() == 0) & (lane == 0)
        ty_low = column(tyc, (x,), 0)
        for y in range(CY):
            here = column(tzc, (x,), y + 1)
            below = jnp.where(start, 0.0, layer_below(tzc, (x,), y + 1, here, lane))
            tzm[x, pl.ds(8 * y, 8), :] = below
            ty_here = column(tyc, (x,), y + 1)
            diag[x, pl.ds(8 * y, 8), :] = (
                column(diag, (x,), y) + (column(txc, (x + 1,), y) + column(txc, (x,), y))
                + (ty_here + ty_low) + (here + below)
            )
            ty_low = ty_here
        return 0

    lax.fori_loop(0, CX, diagonal, 0)

    def split(v):
        high = v.astype(BF16).astype(F32)
        return high, (v - high)

    def terms(t, _):
        lane = lanes().astype(F32)
        at = pl.ds(pl.multiple_of(16 * t, 16), 16)
        high, low = [], []
        for half in range(2):
            tile = in2[pl.ds(pl.multiple_of(16 * t + 8 * half, 8), 8), :]
            total = [jnp.zeros((8, 128), F32) for _ in range(8)]
            for p in range(PERF):
                value = jnp.broadcast_to(tile[:, p : p + 1], (8, 128))
                layer = jnp.broadcast_to(tile[:, 16 + p : 17 + p], (8, 128))
                for c in range(8):
                    total[c] = total[c] + jnp.where(layer == lane + 128.0 * c, value, 0.0)
            total = jnp.concatenate(total, axis=1)
            h, l = split(total)
            high.append(h)
            low.append(l)
        high = jnp.concatenate(high, axis=0).astype(BF16)
        right[at, :] = high
        right[pl.ds(pl.multiple_of(128 + 16 * t, 16), 16), :] = jnp.concatenate(low, axis=0).astype(BF16)
        right[pl.ds(pl.multiple_of(256 + 16 * t, 16), 16), :] = high
        return 0

    def arrived(source):
        d = lax.rem(gx + NGX - source, NGX)
        remote(out2.at[0], in2.at[pl.ds(source * NGY, NGY)], s2.at[d], r2.at[d], "gx", source).wait_recv()

    arrived(gx + 1 - 2 * lax.rem(gx, 2))
    terms(gx // 2, 0)

    def next_tile(j, _):
        i = j // 2
        t = 2 * lax.rem(gx // 4 + i * (i + 1) // 2, 4) + lax.rem(lax.rem(gx, 4) // 2 + j, 2)
        arrived(2 * t)
        arrived(2 * t + 1)
        return terms(t, 0)

    lax.fori_loop(1, NGX // 2, next_tile, 0)
    for c in second:
        c.wait_send()


    def block(x):
        if isinstance(x, int):
            return K * CY * (0 if x == 0 else 1 if x == CX - 1 else x + 1)
        return pl.multiple_of(K * CY * (x + 1), K * CY)

    across = in2[...].T

    mis_high, mis_low = split(across[32:36, :])
    for x in range(CX):
        spot = (lax.broadcasted_iota(jnp.int32, (CY, 128), 0) + CY * x).astype(F32) == across[36:37, :]
        for k in RHS:
            at = pl.ds(block(x) + CY * k, CY)
            high = jnp.where(spot, mis_high[k : k + 1, :], 0.0).astype(BF16)
            left[at, 0:128] = high
            left[at, 128:256] = high
            left[at, 256:384] = jnp.where(spot, mis_low[k : k + 1, :], 0.0).astype(BF16)

    def gather(part):
        def at(n, _):
            here = pl.ds(pl.multiple_of(256 * n, 256), 256)
            src[part, here] = jnp.dot(left[part, :], right[:, here], preferred_element_type=F32)
            return 0
        lax.fori_loop(0, NZ // 256, at, 0)

    for c in fields:
        c.wait()

    def begin(x):
        for k in RHS:
            for t in range(2):
                for c in range(8):
                    at = (pl.ds(8 * t, 8), pl.ds(128 * c, 128))
                    row = block(x) + (CY * k + 8 * t)
                    row = row if isinstance(x, int) else pl.multiple_of(row, 8)
                    v = co[3, x, *at] * na[k, x, *at] + src[pl.ds(row, 8), pl.ds(128 * c, 128)]
                    b[k, x + 1, pl.ds(8 + 64 * t + c, 8, stride=8), :] = v

    def face(src_ref, dst_ref, at, axis, to):
        return remote(src_ref, dst_ref, hs.at[at], hr.at[at], axis, to)

    low, high = pl.ds(8, 8), pl.ds(8 * CY, 8)
    before, after = pl.ds(0, 8), pl.ds(8 * CY + 8, 8)

    def loop(lo, hi, fn):
        def body(x, _):
            fn(x)
            return 0
        lax.fori_loop(lo, hi, body, 0)

    def apply(v, put, x, ys, sums, halo=True, dots=True):
        lane = lanes()
        sums = list(sums)
        prev = None
        for y in ys:
            cols = (x - 1,)
            d = column(diag, cols, y - 1)
            txp, txl = column(txc, (x,), y - 1), column(txc, (x - 1,), y - 1)
            typ = column(tyc, cols, y)
            tzp, tzl = column(tzc, cols, y), column(tzm, cols, y - 1)
            if prev is None or prev[0] != y - 1:
                prev = (y - 1, column(tyc, cols, y - 1), [column(v, (k, x), y - 1) if halo or y > 1 else None for k in RHS],
                        [column(v, (k, x), y) for k in RHS])
            _, tyl, down, mid = prev
            up = [column(v, (k, x), y + 1) if halo or y < CY else None for k in RHS]
            for k in RHS:
                here = mid[k]
                out = d * here
                if halo or not (isinstance(x, int) and x == CX):
                    out = out - txp * column(v, (k, x + 1), y)
                if halo or not (isinstance(x, int) and x == 1):
                    out = out - txl * column(v, (k, x - 1), y)
                if up[k] is not None:
                    out = out - typ * up[k]
                if down[k] is not None:
                    out = out - tyl * down[k]
                out = out - (tzp * layer_above(v, (k, x), y, here, lane) + tzl * layer_below(v, (k, x), y, here, lane))
                put(k, x, y, out)
                if dots:
                    sums[k] = sums[k] + here * here
                    sums[K + k] = sums[K + k] + here * out
            prev = (y, typ, mid, up)
        return tuple(sums)

    def put_q(k, x, y, out):
        q[k, x, pl.ds(8 * y, 8), :] = out

    def put_end(k, x, y, out):
        put_q(k, x, y, out)
        if y in (1, CY):
            return
        send_x[0 if x == 1 else 1, k, pl.ds(8 * (y - 1), 8), :] = out

    def put_side(k, x, y, out):
        put_q(k, x, y, out)
        send_y[0 if y == 1 else 1, k, x - 1] = out

    def put_w(k, x, y, out):
        w[k, x - 1, pl.ds(8 * (y - 1), 8), :] = out

    def ends(v, put, sums, **kw):
        for x in (1, CX):
            sums = apply(v, put, x, range(1, CY + 1), sums, **kw)
        return sums

    def sides(v, put, sums, **kw):
        def at(i, s):
            for j in range(7):
                s = apply(v, put, 2 + 7 * i + j, (1, CY), s, **kw)
            return s
        return lax.fori_loop(0, 2, at, sums)

    none = tuple(jnp.zeros((8, 128), F32) for _ in range(2 * K))
    planes = pl.ds(8, 8 * CY)
    inside_y = pl.ds(16, 8 * (CY - 2))
    inside_x = pl.ds(2, CX - 2)
    all_x = pl.ds(1, CX)

    both = ((1, CX + 1, 0, 0, down_x), (CX, 0, 1, CX, up_x))
    both_y = ((low, after, 0, 1, down_y), (high, before, 1, CY, up_y))

    gather(pl.ds(0, 2 * K * CY))
    begin(0)
    begin(CX - 1)
    tips = []
    for i, (x, to_x, _, _, x_axis) in enumerate(both):
        for j, (y, to_y, _, _, y_axis) in enumerate(both_y):
            at = 10 + 4 * i + 2 * j
            tips.append(face(b.at[:, x, y], b.at[:, to_x, y], at, "gx", x_axis))
            tips.append(face(b.at[:, x, y], b.at[:, x, to_y], at + 1, "gy", y_axis))
    for c in tips:
        c.start()
    bx = [face(b.at[:, x, inside_y], b.at[:, to_x, inside_y], 2 + i, "gx", axis)
          for i, (x, to_x, _, _, axis) in enumerate(both)]
    for c in bx:
        c.start()
    by = []
    for part, some in enumerate((range(1, CX // 2), range(CX // 2, CX - 1))):
        gather(pl.ds(block(some[0]), len(some) * K * CY))
        loop(some[0], some[-1] + 1, begin)
        here = pl.ds(some[0] + 1, len(some))
        for i, (y, to_y, _, _, axis) in enumerate(both_y):
            c = face(b.at[:, here, y], b.at[:, here, to_y], (4 if part == 0 else 22) + i, "gy", axis)
            c.start()
            by.append(c)

    ends(b, put_end, none, halo=False, dots=False)
    sides(b, put_side, none, halo=False, dots=False)
    for c in tips:
        c.wait()
    for x, _, i, x_edge, _ in both:
        for _, _, j, y, _ in both_y:
            for k in RHS:
                here = column(q, (k, x), y)
                far_y = column(tyc, (x - 1,), 0 if y == 1 else CY) * column(b, (k, x), 0 if y == 1 else CY + 1)
                far_x = column(txc, (x_edge,), y - 1) * column(b, (k, 0 if x == 1 else CX + 1), y)
                send_x[i, k, pl.ds(8 * (y - 1), 8), :] = here - far_y
                send_y[j, k, x - 1] = here - far_x
    qy = [face(send_y.at[j], q.at[:, all_x, to_y], 8 + j, "gy", axis)
          for j, (_, to_y, _, _, axis) in enumerate(both_y)]
    for c in qy:
        c.start()
    first_half, second_half = [], []
    for i, (_, to_x, _, _, axis) in enumerate(both):
        for half in range(2):
            ks = pl.ds(2 * half, 2)
            c = face(send_x.at[i, ks], q.at[ks, to_x, planes], 18 + 2 * i + half, "gx", axis)
            (second_half if i == half else first_half).append(c)
    one = lax.fori_loop(2, 6, lambda x, s: apply(b, put_q, x, range(2, CY), s), none)
    for c in first_half:
        c.start()
    one = lax.fori_loop(6, CX, lambda x, s: apply(b, put_q, x, range(2, CY), s), one)

    two = lax.fori_loop(3, CX - 1, lambda x, s: apply(q, put_w, x, range(3, CY - 1), s), none)

    def complete(x, y, sums):
        sums = list(sums)
        for k in RHS:
            here = column(b, (k, x), y)
            out = column(q, (k, x), y)
            if isinstance(x, int):
                edge = 0 if x == 1 else CX
                out = out - column(txc, (edge,), y - 1) * column(b, (k, 0 if x == 1 else CX + 1), y)
            if y == 1:
                out = out - column(tyc, (x - 1,), 0) * column(b, (k, x), 0)
            if y == CY:
                out = out - column(tyc, (x - 1,), CY) * column(b, (k, x), CY + 1)
            put_q(k, x, y, out)
            sums[k] = sums[k] + here * here
            sums[K + k] = sums[K + k] + here * out
        return tuple(sums)

    for c in by + bx:
        c.wait()
    for x in (1, CX):
        for y in range(1, CY + 1):
            one = complete(x, y, one)
    one = lax.fori_loop(2, CX, lambda x, s: complete(x, CY, complete(x, 1, s)), one)
    for c in second_half:
        c.start()

    def ring(i, s):
        for j in range(4):
            s = apply(q, put_w, 3 + 4 * i + j, (1, 2, CY - 1, CY), s, halo=False)
        return s

    two = lax.fori_loop(0, (CX - 4) // 4, ring, two)
    for x in (1, 2, CX - 1, CX):
        two = apply(q, put_w, x, range(1, CY + 1), two, halo=False)

    def meet(k, x, y, t, far, sums):
        other = t * (far - t * column(b, (k, x), y))
        at = (k, x - 1, pl.ds(8 * (y - 1), 8), slice(None))
        w[at] = w[at] - other
        if sums is not None:
            sums[K + k] = sums[K + k] - 2.0 * (column(q, (k, x), y) * other)

    def meet_x(i, ks, sums):
        x, x_far, edge = ((1, 0, 0), (CX, CX + 1, CX))[i]
        for y in range(1, CY + 1):
            t = column(txc, (edge,), y - 1)
            for k in ks:
                meet(k, x, y, t, column(q, (k, x_far), y), sums)

    def meet_y(y, x, sums):
        t = column(tyc, (x - 1,), 0 if y == 1 else CY)
        for k in RHS:
            meet(k, x, y, t, column(q, (k, x), 0 if y == 1 else CY + 1), sums)

    for c in qy:
        c.wait()

    def lower_y(i, sums):
        sums = list(sums)
        for j in range(4):
            meet_y(1, 1 + 4 * i + j, sums)
        return tuple(sums)

    two = list(lax.fori_loop(0, CX // 4, lower_y, two))
    for c in first_half:
        c.wait()
    meet_x(0, (0, 1), two)
    meet_x(1, (2, 3), two)
    two = tuple(two)

    lane1 = lax.broadcasted_iota(jnp.int32, (1, 128), 1)
    line = jnp.zeros((1, 128), F32)
    for i, s in enumerate(one + two):
        line = jnp.where(lane1 == i, jnp.sum(s, keepdims=True), line)
    red_out[0] = line
    red1[gx] = line
    hops = []
    for d in range(1, NGX):
        to = lax.rem(gx + d, NGX)
        hops.append(remote(red_out.at[0], red1.at[gx], as1.at[d], ar1.at[d], "gx", to))
    for c in hops:
        c.start()
    loop(1, CX + 1, lambda x: meet_y(CY, x, None))
    for c in second_half:
        c.wait()
    meet_x(0, (2, 3), None)
    meet_x(1, (0, 1), None)
    for c in hops:
        c.wait()
    line = jnp.sum(red1[...], axis=0)
    red_out[1] = line
    red2[gy] = line
    hops = []
    for d in range(1, NGY):
        to = lax.rem(gy + d, NGY)
        hops.append(remote(red_out.at[1], red2.at[gy], as2.at[d], ar2.at[d], "gy", to))
    for c in hops:
        c.start()
    for c in hops:
        c.wait()
    line = jnp.sum(red2[...], axis=0)

    rr = line
    bq = pltpu.roll(line, 128 - K, 1)
    qq = pltpu.roll(line, 128 - 2 * K, 1)
    qw = pltpu.roll(line, 128 - 3 * K, 1)
    step0 = rr / bq
    rr1 = step0 * step0 * qq - rr
    grow = 1.0 + rr1 / rr
    step1 = rr1 / (grow * grow * bq - 2.0 * grow * step0 * qq + step0 * step0 * qw)
    sp[0] = step0 + step1 * grow
    sp[1] = step0 * step1


def last_kernel(b, q, w, sp, x_h, r_h, xo, ro, sem):
    ones = [jnp.broadcast_to(sp[0][:, k : k + 1], (8, 128)) for k in RHS]
    twos = [jnp.broadcast_to(sp[1][:, k : k + 1], (8, 128)) for k in RHS]
    copies = []
    step = 2

    def at(x, _):
        for k in RHS:
            for t in range(2):
                for c in range(8):
                    bv = b[k, x + 1, pl.ds(8 + 64 * t + c, 8, stride=8), :]
                    qv = q[k, x + 1, pl.ds(8 + 64 * t + c, 8, stride=8), :]
                    wv = w[k, x, pl.ds(64 * t + c, 8, stride=8), :]
                    to = (k, x, pl.ds(8 * t, 8), pl.ds(128 * c, 128))
                    xo[to] = ones[k] * bv - twos[k] * qv
                    ro[to] = bv - ones[k] * qv + twos[k] * wv
        return 0

    for i in range(CX // step):
        lax.fori_loop(i * step, (i + 1) * step, at, 0)
        part = pl.ds(i * step, step)
        for j, (s, h) in enumerate(((xo, x_h), (ro, r_h))):
            c = pltpu.make_async_copy(s.at[:, part], h.at[:, part], sem.at[2 * i + j])
            c.start()
            copies.append(c)
    for c in copies:
        c.wait()


def body(next_adjoint, accumulation, trans_x, trans_y, trans_z,
         well_owner, well_site, perf_layers, perf_count, well_index, misfit):
    dma = pltpu.SemaphoreType.DMA
    vm = pltpu.VMEM
    field = (K, CX + 2, 8 * (CY + 2), 128)
    plane = (CX, 8 * CY, 128)
    anywhere = pl.BlockSpec(memory_space=pl.ANY)
    inside = pl.BlockSpec(memory_space=pltpu.VMEM)
    b, q, w, sp = pl.pallas_call(
        main_kernel,
        out_shape=(
            pltpu.VMEM(field, F32), pltpu.VMEM(field, F32), pltpu.VMEM((K, *plane), F32), pltpu.VMEM((2, 1, 128), F32),
        ),
        in_specs=[anywhere] * 11,
        out_specs=(inside,) * 4,
        scratch_shapes=[
            vm((K, CX, CY, NZ), F32), vm((4, CX, CY, NZ), F32), vm((K * CX * CY, NZ), F32),
            vm(plane, F32), vm((CX + 1, 8 * CY, 128), F32), vm((CX, 8 * CY + 8, 128), F32),
            vm((CX, 8 * CY + 8, 128), F32), vm(plane, F32),
            vm((1, WELLS), jnp.int32), vm((1, WELLS), jnp.int32), vm((PERF, WELLS), jnp.int32),
            vm((1, WELLS), jnp.int32), vm((PERF, WELLS), F32), vm((K, WELLS), F32),
            vm((128, WELLS), F32), vm((NGY, NGX, 128), F32), vm((NGY * NGX, 128), F32),
            vm((NGX, NGY, 128), F32), vm((NGX * NGY, 128), F32),
            vm((K * CX * CY, 384), BF16), vm((384, NZ), BF16),
            vm((2, K, 8 * CY, 128), F32), vm((2, K, CX, 8, 128), F32),
            vm((2, 1, 128), F32), vm((NGX, 1, 128), F32), vm((NGY, 1, 128), F32),
            dma((8,)), dma((6,)), dma((NGY,)), dma((NGY,)), dma((NGX,)), dma((NGX,)),
            dma((24,)), dma((24,)), dma((NGX,)), dma((NGX,)), dma((NGY,)), dma((NGY,)),
        ],
        compiler_params=pltpu.CompilerParams(
            collective_id=0, has_side_effects=True, vmem_limit_bytes=40 * 2**20),
        cost_estimate=pl.CostEstimate(flops=60_000_000, bytes_accessed=9_000_000, transcendentals=0),
        name="adjoint_krylov",
    )(next_adjoint, accumulation, trans_x, trans_y, trans_z, well_owner.T, well_site.reshape(1, WELLS),
      perf_layers.T, perf_count.reshape(1, WELLS), well_index.T, misfit.T)
    out = jax.ShapeDtypeStruct((K, CX, CY, NZ), F32)
    return pl.pallas_call(
        last_kernel,
        out_shape=(out, out),
        in_specs=[inside] * 4,
        out_specs=(anywhere, anywhere),
        scratch_shapes=[vm((K, CX, CY, NZ), F32), vm((K, CX, CY, NZ), F32), dma((16,))],
        compiler_params=pltpu.CompilerParams(vmem_limit_bytes=24 * 2**20),
        name="adjoint_result",
    )(b, q, w, sp)


def solution(mesh):
    flat = P(("gx", "gy"))
    rows_of = P(("gx", "gy"), None)
    cells = P("gx", "gy", None)
    many = P(None, "gx", "gy", None)
    return jax.shard_map(
        body,
        mesh=mesh,
        in_specs=(many, cells, cells, cells, cells, rows_of, flat, rows_of, flat, rows_of, rows_of),
        out_specs=(many, many),
        check_vma=False,
    )
```
